32 devices in a mesh: pts: 8 (over z, x), rhs: 4 (over y, core).
Axes of the slice: x: 2, y: 2, z: 4, core: 2. Of those that a mesh axis runs over, the one named last changes fastest.
Arguments:
- points: bfloat16 [16384, 32], P('pts'), may hold values from -0.5 to 0.5
- noise_var: float32 [16384], P('pts'), may hold values from 0.5 to 0.6
- right_side: float32 [64, 16384], P('rhs', 'pts'), may hold values from -12 to 12
- pattern: int32 [128, 33], P('pts'), may hold values from 0 to 1, as said below
Outputs:
- solution: float32 [64, 16384], P('rhs', 'pts')
- residual: float32 [64, 16384], P('rhs', 'pts')
- res_image: float32 [64, 16384], P('rhs', 'pts')
The draws below stay inside these ranges and needn't reach their ends.
Inputs may be any that keep to these rules, and one draw needn't show every extreme that they name: Symmetric: pattern[b, 16 + d] = pattern[b + d, 16 - d]; the centre column is 1; entries naming a block outside 0 to 127 are 0.
All inputs are finite; a program needn't handle non-finite values.
Results may differ from the reference program's by a relative error of at most 0.0036.
Values may be sent and summed in bfloat16 or wider, within the bound.
No kernel may reach another device: no remote copies, remote signals or barrier semaphores. Data moves between devices by JAX's collectives and lax.ppermute only.
A program may use at most 64 MiB of HBM per device.

```python
import math
import jax
import jax.numpy as jnp
from jax import lax

F = 32
R = 64
BLK = 128
REACH = 16
ITERS = 2
BLK_DEV = 16
WIDE = 33
WEXP = 18
NBLK = 128
POINTS = 16384


def draw_points(key, part):
    first_key, second_key, third_key = jax.random.split(key, 3)
    freqs = jax.random.uniform(first_key, (F // 2,), jnp.float32, 0.002, 0.004)
    position = jnp.arange(POINTS, dtype=jnp.float32) / BLK
    angles = position[:, None] * freqs[None, :]
    centre = 0.25 * jnp.concatenate([jnp.cos(angles), jnp.sin(angles)], axis=1)
    rough = jnp.exp(jax.random.uniform(second_key, (POINTS, 1), jnp.float32, math.log(0.5), math.log(2.0)))
    jitter = jax.random.truncated_normal(third_key, -4.0, 4.0, (POINTS, F), jnp.float32)
    return (centre + 0.02 * rough * jitter).astype(jnp.bfloat16)


def draw_right_side(key, part):
    first_key = jax.random.fold_in(key, 0)
    scales = 1.0 + 2.0 * jnp.arange(POINTS, dtype=jnp.float32) / POINTS
    values = jax.random.truncated_normal(first_key, -4.0, 4.0, (R, POINTS), jnp.float32)
    return values * scales[None, :]


def draw_pattern(key, part):
    first_key, second_key = jax.random.split(key, 2)
    thresholds = jax.random.randint(first_key, (NBLK // BLK_DEV,), 3, 13)
    raw_bits = jax.random.randint(second_key, (NBLK, REACH), 0, 16)
    block_ids = jnp.arange(NBLK, dtype=jnp.int32)
    inside = block_ids[:, None] + jnp.arange(1, REACH + 1, dtype=jnp.int32)[None, :] < NBLK
    upper = ((raw_bits < thresholds[block_ids // BLK_DEV][:, None]) & inside).astype(jnp.int32)
    columns = []
    for distance in range(REACH, 0, -1):
        columns.append(jnp.concatenate([jnp.zeros((distance,), jnp.int32), upper[:NBLK - distance, distance - 1]]))
    columns.append(jnp.ones((NBLK,), jnp.int32))
    for distance in range(1, REACH + 1):
        columns.append(upper[:, distance - 1])
    return jnp.stack(columns, axis=1)


def steps_of(own_key, shape, cuts, low, high):
    def one(axis_at, parts):
        steps = jax.random.uniform(jax.random.fold_in(jax.random.fold_in(own_key, 6), axis_at), (parts,), jnp.float32, low / len(cuts), high / len(cuts))
        return jnp.repeat(jnp.exp(steps), shape[axis_at] // parts).reshape((-1,) + (1,) * (len(shape) - axis_at - 1))

    loudness = one(*cuts[0])
    for cut in cuts[1:]:
        loudness = loudness * one(*cut)
    return loudness


def setup_inputs(seed: int = 0) -> dict:
    seeds = jax.random.split(jax.random.key(seed), 5)
    points = draw_points(jax.random.fold_in(seeds[4], 71), 0)
    noise_var = jnp.clip(0.5 + 0.100000024 * jax.random.uniform(seeds[1], (POINTS,), jnp.float32) ** steps_of(seeds[1], (POINTS,), ((0, 8),), -0.2, 0.2), 0.5, 0.6)
    right_side = draw_right_side(jax.random.fold_in(seeds[4], 71), 0)
    pattern = draw_pattern(jax.random.fold_in(seeds[4], 71), 0)
    return dict(points=points, noise_var=noise_var, right_side=right_side, pattern=pattern)


def kernel_block(left_points, right_points, left_squares, right_squares):
    cross_terms = jnp.einsum('gif,gjf->gij', left_points, right_points, precision=lax.Precision.HIGHEST)
    dist_squared = jnp.maximum(left_squares[:, :, None] + right_squares[:, None, :] - 2.0 * cross_terms, 0.0)
    radius = jnp.sqrt(dist_squared)
    return jnp.maximum(1.0 - radius, 0.0) ** WEXP * (WEXP * radius + 1.0)

def reference(points, noise_var, right_side, pattern):
    point_blocks = points.astype(jnp.float32).reshape(NBLK, BLK, F)
    squares = lax.optimization_barrier(jnp.sum(point_blocks * point_blocks, axis=2))
    padded_points = jnp.pad(point_blocks, ((REACH, REACH), (0, 0), (0, 0)))
    padded_squares = jnp.pad(squares, ((REACH, REACH), (0, 0)))
    kernel_scale = 1.0 / (4 * BLK)

    def apply_operator(vector):
        vec_low = lax.optimization_barrier(vector.astype(jnp.bfloat16))
        vec_blocks = jnp.pad(vec_low.astype(jnp.float32).T.reshape(NBLK, BLK, R), ((REACH, REACH), (0, 0), (0, 0)))

        def one_offset(running, offset):
            other_points = lax.dynamic_slice_in_dim(padded_points, offset, NBLK, 0)
            other_squares = lax.dynamic_slice_in_dim(padded_squares, offset, NBLK, 0)
            other_vec = lax.dynamic_slice_in_dim(vec_blocks, offset, NBLK, 0)
            profile = kernel_block(point_blocks, other_points, squares, other_squares)
            pattern_col = lax.dynamic_index_in_dim(pattern, offset, 1, keepdims=False).astype(jnp.float32)
            weights_low = lax.optimization_barrier((profile * pattern_col[:, None, None]).astype(jnp.bfloat16))
            weights = weights_low.astype(jnp.float32)
            running = running + jnp.einsum('gij,gjc->gic', weights, other_vec, precision=lax.Precision.HIGHEST)
            return (running, offset)
        summed = lax.scan(one_offset, jnp.zeros((NBLK, BLK, R), jnp.float32), jnp.arange(WIDE, dtype=jnp.int32))[0]
        return noise_var[None, :] * vector + kernel_scale * summed.reshape(POINTS, R).T
    solution = jnp.zeros_like(right_side)
    residual = right_side
    res_image = apply_operator(residual)
    direction = jnp.zeros_like(right_side)
    dir_image = jnp.zeros_like(right_side)
    dir_twice = jnp.zeros_like(right_side)
    norm_prev = None
    step_prev = None
    for iteration in range(ITERS):
        norm_now = lax.optimization_barrier(jnp.sum(residual * residual, axis=1))[:, None]
        curvature = lax.optimization_barrier(jnp.sum(res_image * residual, axis=1))[:, None]
        square_image = apply_operator(res_image)
        if iteration == 0:
            step_len = norm_now / curvature
            direction = residual
            dir_image = res_image
            dir_twice = square_image
        else:
            mix_ratio = norm_now / norm_prev
            step_len = norm_now / (curvature - mix_ratio * norm_now / step_prev)
            direction = residual + mix_ratio * direction
            dir_image = res_image + mix_ratio * dir_image
            dir_twice = square_image + mix_ratio * dir_twice
        solution = solution + step_len * direction
        residual = residual - step_len * dir_image
        res_image = res_image - step_len * dir_twice
        norm_prev = norm_now
        step_prev = step_len
    return (solution, residual, res_image)
```

```python
import functools

import jax
import jax.numpy as jnp
from jax import lax
from jax.experimental import pallas as pl
from jax.experimental.pallas import tpu as pltpu
from jax.sharding import PartitionSpec as P

F = 32
BLK = 128
REACH = 16
WIDE = 33
WEXP = 18
LANES = 128
PACK = LANES // F
GAMMA = float(WEXP) ** (1.0 / (WEXP + 1))
GAMMA_SQ = GAMMA * GAMMA
OFFSET = GAMMA * (WEXP + 1) / WEXP
TINY = 1e-30
SHIFT = 2.0 / (0.5 + 0.6)
SUMS = 9
UNROLL = 4
MIB = 1 << 20

f32 = jnp.float32
bf16 = jnp.bfloat16


def rounded(x):
    return x.astype(bf16).astype(f32)


def three_parts(x):
    high = rounded(x)
    rest = x - high
    middle = rounded(rest)
    return high, middle, rounded(rest - middle)


def spread_features(packed, group):
    source = lax.broadcasted_iota(jnp.int32, (LANES, LANES), 0)
    target = lax.broadcasted_iota(jnp.int32, (LANES, LANES), 1)
    pick = (source == group * F + target % F) & (target < 3 * F)
    return jnp.dot(packed, pick.astype(bf16), preferred_element_type=f32)


def square_parts(features, lane):
    squares = jnp.sum(jnp.where(lane < F, features * features, 0.0), axis=1, keepdims=True)
    return three_parts(GAMMA_SQ * squares)


def left_features(features, lane, parts):
    out = jnp.where(lane < 3 * F, features, jnp.where(lane < 3 * F + 6, 1.0, 0.0))
    for at, part in enumerate(parts):
        out = jnp.where(lane == 3 * F + at, part, out)
    return out


def right_features(features, lane, parts):
    high, middle, low = three_parts((-2.0 * GAMMA_SQ) * features)
    out = jnp.where(lane < F, high, jnp.where(lane < 2 * F, middle, jnp.where(lane < 3 * F, low, 0.0)))
    out = jnp.where((lane >= 3 * F) & (lane < 3 * F + 3), 1.0, out)
    for at, part in enumerate(parts):
        out = jnp.where(lane == 3 * F + 3 + at, part, out)
    return out


def fill_features(packed, left_ref, right_ref):
    rows = packed.shape[0]
    per = rows // BLK
    lane = lax.broadcasted_iota(jnp.int32, (rows, LANES), 1)
    for group in range(PACK):
        features = spread_features(packed, group)
        parts = square_parts(features, lane)
        left = left_features(features, lane, parts).astype(bf16)
        for at in range(per):
            left_ref[group * per + at] = left[at * BLK : (at + 1) * BLK]
        if right_ref is not None:
            right = right_features(features, lane, parts)
            for at in range(per):
                right_ref[group * per + at] = right[at * BLK : (at + 1) * BLK].T.astype(bf16)


def tile_values(left, right):
    scaled = jnp.dot(left, right, preferred_element_type=f32)
    scaled = jnp.maximum(scaled, TINY)
    s = jnp.maximum(GAMMA - scaled * lax.rsqrt(scaled), 0.0)
    s2 = s * s
    s4 = s2 * s2
    s8 = s4 * s4
    s16 = s8 * s8
    return ((s16 * s2) * (OFFSET - s)).astype(bf16)


def make_tiles(count, list_ref, left_ref, right_ref, tiles_ref):
    def step(at, carry):
        for k in range(UNROLL):
            entry = list_ref[at * UNROLL + k]
            slot = entry & 1023
            other = (entry >> 10) & 63
            home = entry >> 16
            tiles_ref[slot] = tile_values(left_ref[other], right_ref[home])
        return carry

    lax.fori_loop(0, (count + UNROLL - 1) // UNROLL, step, 0)


def list_tiles(blocks, low, high, shift, pattern_ref, list_ref, spare):
    def per_home(home, count):
        def per_other(other, count):
            column = other - home + shift
            slot = home * WIDE + column
            list_ref[count] = (((home << 6) + other) << 10) + slot
            return count + pattern_ref[home, column]

        return lax.fori_loop(low(home), high(home), per_other, count)

    count = lax.fori_loop(0, blocks, per_home, 0)
    for k in range(UNROLL - 1):
        list_ref[count + k] = spare
    return count


def prep_kernel(points_ref, vec_ref, out_ref):
    rows = points_ref.shape[0] // PACK
    out_ref[:rows, :] = jnp.concatenate(
        [points_ref[g * rows : (g + 1) * rows, :] for g in range(PACK)], axis=1
    )
    put_blocks(vec_ref[...].astype(bf16), out_ref, rows)


def put_blocks(values, out_ref, first):
    width = values.shape[0]
    for b in range(values.shape[1] // BLK):
        out_ref[first + b * width : first + (b + 1) * width, :] = values[:, b * BLK : (b + 1) * BLK]


def local_kernel(blocks, pattern_ref, own_ref, tiles_ref, right_ref, left_ref, list_ref, dead_ref):
    rows = blocks * BLK // PACK
    spare = blocks * WIDE

    def scan(home, count):
        def per_column(column, count):
            slot = home * WIDE + column
            dead_ref[count] = slot
            return count + 1 - pattern_ref[home, column]

        return lax.fori_loop(0, WIDE, per_column, count)

    dead = lax.fori_loop(0, blocks, scan, 0)

    def clear(at, carry):
        tiles_ref[dead_ref[at]] = jnp.zeros((BLK, BLK), bf16)
        return carry

    lax.fori_loop(0, dead, clear, 0)
    fill_features(own_ref[:rows, :], left_ref, right_ref)
    count = list_tiles(
        blocks, lambda a: 0, lambda a: blocks, REACH, pattern_ref, list_ref, spare
    )
    make_tiles(count, list_ref, left_ref, right_ref, tiles_ref)


def side_kernel(blocks, before_ref, pattern_ref, other_ref, right_ref, tiles_in, tiles_ref, left_ref, list_ref):
    del tiles_in
    rows = blocks * BLK // PACK
    spare = blocks * WIDE
    before = before_ref[0]
    fill_features(other_ref[:rows, :], left_ref, None)
    count = list_tiles(
        blocks,
        lambda a: a * before,
        lambda a: jnp.where(before == 1, blocks, a + 1),
        jnp.where(before == 1, 0, 2 * REACH),
        pattern_ref,
        list_ref,
        spare,
    )
    make_tiles(count, list_ref, left_ref, right_ref, tiles_ref)


def gather_wide(blocks, width, first, before, own, side_a, side_b, wide_ref):
    at_a = jnp.where(before == 1, 0, 2 * blocks)
    at_b = 2 * blocks - at_a
    size = blocks * width
    wide_ref[blocks : 2 * blocks] = own[first : first + size].reshape(blocks, width, LANES)
    wide_ref[pl.ds(at_a, blocks)] = side_a[first : first + size].reshape(blocks, width, LANES)
    wide_ref[pl.ds(at_b, blocks)] = side_b[first : first + size].reshape(blocks, width, LANES)


def products(home, wide_ref, tiles_ref):
    vec = jnp.concatenate([wide_ref[home + o] for o in range(WIDE)], axis=1)
    tiles = tiles_ref[home * WIDE : (home + 1) * WIDE].reshape(WIDE * BLK, BLK)
    return jnp.dot(vec, tiles, preferred_element_type=f32)


def first_kernel(blocks, before_ref, own_ref, a_ref, b_ref, tiles_ref, noise_ref, vec_ref, image_ref, low_ref, wide_ref):
    width = vec_ref.shape[0]
    first = blocks * BLK // PACK
    gather_wide(blocks, width, first, before_ref[0], own_ref, a_ref, b_ref, wide_ref)
    for home in range(blocks):
        cols = slice(home * BLK, (home + 1) * BLK)
        image = noise_ref[:, cols] * vec_ref[:, cols] + products(home, wide_ref, tiles_ref) * (1.0 / (4 * BLK))
        image_ref[:, cols] = image
        low_ref[home * width : (home + 1) * width, :] = image.astype(bf16)


def second_kernel(
    blocks, before_ref, own_ref, a_ref, b_ref, tiles_ref, noise_ref, vec_ref, image_ref, twice_ref, low_ref, sums_ref, wide_ref
):
    width = vec_ref.shape[0]
    gather_wide(blocks, width, 0, before_ref[0], own_ref, a_ref, b_ref, wide_ref)
    totals = [jnp.zeros((width, BLK), f32) for _ in range(SUMS)]
    for home in range(blocks):
        cols = slice(home * BLK, (home + 1) * BLK)
        r = vec_ref[:, cols]
        w = image_ref[:, cols]
        q = noise_ref[:, cols] * w + products(home, wide_ref, tiles_ref) * (1.0 / (4 * BLK))
        twice_ref[:, cols] = q
        u = r - SHIFT * w
        y = w - SHIFT * q
        low_ref[2 * home * width : (2 * home + 1) * width, :] = y.astype(bf16)
        low_ref[(2 * home + 1) * width : (2 * home + 2) * width, :] = q.astype(bf16)
        terms = (r * r, r * w, u * u, u * w, w * w, y * u, q * u, y * w, q * w)
        totals = [total + term for total, term in zip(totals, terms)]
    lane = lax.broadcasted_iota(jnp.int32, (width, LANES), 1)
    out = jnp.zeros((width, LANES), f32)
    for at, total in enumerate(totals):
        out = jnp.where(lane == at, jnp.sum(total, axis=1, keepdims=True), out)
    sums_ref[...] = out


def third_kernel(blocks, before_ref, own_ref, a_ref, b_ref, tiles_ref, out_ref, wide_ref):
    width = out_ref.shape[0]
    gather_wide(blocks, width, 0, before_ref[0], own_ref, a_ref, b_ref, wide_ref)
    for home in range(blocks):
        out_ref[:, home * BLK : (home + 1) * BLK] = products(home, wide_ref, tiles_ref) * (1.0 / (4 * BLK))


def last_kernel(sums_ref, noise_ref, vec_ref, image_ref, twice_ref, prod_ref, x_ref, r_ref, w_ref):
    width = vec_ref.shape[0]
    rr, rw, uu, uw, ww, yu, qu, yw, qw = [sums_ref[:, at : at + 1] for at in range(SUMS)]
    alpha0 = rr / rw
    delta = alpha0 - SHIFT
    norm = uu - 2.0 * delta * uw + delta * delta * ww
    curv = yu - delta * (qu + yw) + delta * delta * qw
    beta = norm / rr
    alpha1 = norm / (curv - beta * norm / alpha0)
    r0, w0, q0 = vec_ref[...], image_ref[...], twice_ref[...]
    r1 = r0 - alpha0 * w0
    w1 = w0 - alpha0 * q0
    q1 = noise_ref[...] * w1 + (prod_ref[:width, :] - delta * prod_ref[width:, :])
    x_ref[...] = alpha0 * r0 + alpha1 * (r1 + beta * r0)
    r_ref[...] = r1 - alpha1 * (w1 + beta * w0)
    w_ref[...] = w1 - alpha1 * (q1 + beta * q0)


def swap_pairs(count, first):
    pairs = []
    for low in range(first, count - 1, 2):
        pairs += [(low, low + 1), (low + 1, low)]
    return pairs


def both_sides(x):
    count = lax.axis_size("pts")
    return (
        lax.ppermute(x, "pts", swap_pairs(count, 0)),
        lax.ppermute(x, "pts", swap_pairs(count, 1)),
    )


def total_over_points(x):
    count = lax.axis_size("pts")
    if count & (count - 1):
        return lax.psum(x, "pts")
    step = 1
    while step < count:
        x = x + lax.ppermute(x, "pts", [(i, i ^ step) for i in range(count)])
        step *= 2
    return x


def near(x):
    return pltpu.with_memory_space_constraint(x, pltpu.VMEM)


VM = pl.BlockSpec(memory_space=pltpu.VMEM)
SM = pl.BlockSpec(memory_space=pltpu.SMEM)


def cost(flops, moved, special=0):
    return pl.CostEstimate(flops=flops, bytes_accessed=moved, transcendentals=special)


def per_device(points, noise_var, right_side, pattern):
    local_rows = points.shape[0]
    width = right_side.shape[0]
    blocks = local_rows // BLK
    slots = blocks * WIDE + 1
    packed_rows = local_rows // PACK
    list_len = blocks * blocks + UNROLL
    before = (lax.axis_index("pts") % 2).astype(jnp.int32).reshape(1)
    noise = noise_var[None, :]
    params = pltpu.CompilerParams(vmem_limit_bytes=40 * MIB)
    tiles_type = pltpu.VMEM((slots, BLK, BLK), bf16)
    full = (width, local_rows)

    payload = pl.pallas_call(
        prep_kernel,
        out_shape=jax.ShapeDtypeStruct((packed_rows + blocks * width, LANES), bf16),
        in_specs=[VM, VM],
        out_specs=VM,
        name="prep",
    )(points, right_side)
    halo_a, halo_b = both_sides(payload)
    tiles, right = pl.pallas_call(
        functools.partial(local_kernel, blocks),
        out_shape=(tiles_type, pltpu.VMEM((blocks, LANES, BLK), bf16)),
        in_specs=[SM, VM],
        out_specs=(VM, VM),
        scratch_shapes=[
            pltpu.VMEM((blocks, BLK, LANES), bf16),
            pltpu.SMEM((list_len,), jnp.int32),
            pltpu.SMEM((blocks * WIDE + 1,), jnp.int32),
        ],
        compiler_params=params,
        cost_estimate=cost(10**9, 10**7),
        name="local_tiles",
    )(pattern, payload)
    for name, halo in (("tiles_a", halo_a), ("tiles_b", halo_b)):
        tiles = pl.pallas_call(
            functools.partial(side_kernel, blocks),
            out_shape=tiles_type,
            in_specs=[SM, SM, VM, VM, VM],
            out_specs=VM,
            scratch_shapes=[
                pltpu.VMEM((blocks, BLK, LANES), bf16),
                pltpu.SMEM((list_len,), jnp.int32),
            ],
            input_output_aliases={4: 0},
            compiler_params=params,
            cost_estimate=cost(10**9, 10**7),
            name=name,
        )(before if name == "tiles_a" else 1 - before, pattern, halo, near(right), near(tiles))

    def wide(rows):
        return [pltpu.VMEM((3 * blocks, rows, LANES), bf16)]

    image, low = pl.pallas_call(
        functools.partial(first_kernel, blocks),
        out_shape=(jax.ShapeDtypeStruct(full, f32), jax.ShapeDtypeStruct((blocks * width, LANES), bf16)),
        in_specs=[SM] + [VM] * 6,
        out_specs=(VM, VM),
        scratch_shapes=wide(width),
        compiler_params=params,
        name="image",
    )(before, payload, halo_a, halo_b, near(tiles), noise, right_side)
    low_a, low_b = both_sides(low)
    twice, low, sums = pl.pallas_call(
        functools.partial(second_kernel, blocks),
        out_shape=(
            jax.ShapeDtypeStruct(full, f32),
            jax.ShapeDtypeStruct((2 * blocks * width, LANES), bf16),
            jax.ShapeDtypeStruct((width, LANES), f32),
        ),
        in_specs=[SM] + [VM] * 7,
        out_specs=(VM, VM, VM),
        scratch_shapes=wide(width),
        compiler_params=params,
        name="twice",
    )(before, low, low_a, low_b, near(tiles), noise, right_side, image)
    low_a, low_b = both_sides(low)
    sums = total_over_points(sums)
    prods = pl.pallas_call(
        functools.partial(third_kernel, blocks),
        out_shape=jax.ShapeDtypeStruct((2 * width, local_rows), f32),
        in_specs=[SM] + [VM] * 4,
        out_specs=VM,
        scratch_shapes=wide(2 * width),
        compiler_params=params,
        name="products",
    )(before, low, low_a, low_b, near(tiles))
    return pl.pallas_call(
        last_kernel,
        out_shape=tuple(jax.ShapeDtypeStruct(full, f32) for _ in range(3)),
        in_specs=[VM] * 6,
        out_specs=(VM, VM, VM),
        compiler_params=params,
        name="update",
    )(sums, noise, right_side, image, twice, prods)


def solution(mesh):
    placed = (P("pts", None), P("pts"), P("rhs", "pts"), P("pts", None))
    return jax.shard_map(
        per_device,
        mesh=mesh,
        in_specs=placed,
        out_specs=(P("rhs", "pts"), P("rhs", "pts"), P("rhs", "pts")),
        check_vma=False,
    )
```

```python
import functools

import jax
import jax.numpy as jnp
from jax import lax
from jax.experimental import pallas as pl
from jax.experimental.pallas import tpu as pltpu
from jax.sharding import PartitionSpec as P

F = 32
BLK = 128
REACH = 16
WEXP = 18
LANES = 128
GAMMA = float(WEXP) ** (1.0 / (WEXP + 1))
GAMMA_SQ = GAMMA * GAMMA
OFFSET = GAMMA * (WEXP + 1) / WEXP
TINY = 1e-30
SCALE = 1.0 / (4 * BLK)
SHIFT = 2.0 / (0.5 + 0.6)
SUMS = 9
UNROLL = 16
TAIL = 4
FIELD = 9
MIB = 1 << 20

f32 = jnp.float32
bf16 = jnp.bfloat16


def rounded(x):
    return x.astype(bf16).astype(f32)


def three_parts(x):
    high = rounded(x)
    rest = x - high
    middle = rounded(rest)
    return high, middle, rounded(rest - middle)


def eight_rows(rows):
    row = lax.broadcasted_iota(jnp.int32, (8, rows[0].shape[1]), 0)
    out = jnp.zeros((8, rows[0].shape[1]), f32)
    for at, value in enumerate(rows):
        out = jnp.where(row == at, value, out)
    return out


def fill_features(points, left_ref, right_ref):
    x = points.astype(f32)
    count = x.shape[1]
    squares = three_parts(GAMMA_SQ * jnp.sum(x * x, axis=0, keepdims=True))
    ones = [jnp.ones((1, count), f32)] * 3
    blank = jnp.zeros((LANES - 3 * F - 8, count), f32)
    left = jnp.concatenate([x, x, x, eight_rows(list(squares) + ones), blank], axis=0).astype(bf16)
    for b in range(count // BLK):
        left_ref[b] = left[:, b * BLK : (b + 1) * BLK].T
    if right_ref is not None:
        cross = three_parts((-2.0 * GAMMA_SQ) * x)
        right = jnp.concatenate(list(cross) + [eight_rows(ones + list(squares)), blank], axis=0).astype(bf16)
        for b in range(count // BLK):
            right_ref[b] = right[:, b * BLK : (b + 1) * BLK]


def tile_values(left, right):
    scaled = jnp.dot(left, right, preferred_element_type=f32)
    scaled = jnp.maximum(scaled, TINY)
    s = jnp.maximum(GAMMA - scaled * lax.rsqrt(scaled), 0.0)
    s2 = s * s
    s4 = s2 * s2
    s8 = s4 * s4
    s16 = s8 * s8
    return ((s16 * s2) * (OFFSET - s)).astype(bf16)


def entry(slot, mirror, other, home):
    return (((((home << 4) + other) << FIELD) + mirror) << FIELD) + slot


def make_tiles(count, list_ref, left_ref, right_ref, tiles_ref, mirrored):
    mask = (1 << FIELD) - 1

    def one(at):
        code = list_ref[at]
        home = code >> (2 * FIELD + 4)
        other = (code >> (2 * FIELD)) & 15
        tile = tile_values(left_ref[other], right_ref[home])
        if mirrored:
            tiles_ref[(code >> FIELD) & mask] = tile.T
        tiles_ref[code & mask] = tile

    def step(at, carry):
        for k in range(UNROLL):
            one(at * UNROLL + k)
        return carry

    def tail(at, carry):
        for k in range(TAIL):
            one(at * TAIL + k)
        return carry

    whole = count // UNROLL
    lax.fori_loop(0, whole, step, 0)
    lax.fori_loop(whole * (UNROLL // TAIL), (count + TAIL - 1) // TAIL, tail, 0)


def local_slot(blocks, home, other):
    return ((home // 2) * blocks + other) * 2 + home % 2


def side_slot(blocks, home, other, after):
    wide = other - 2 * (home // 2) + (blocks if after else 0)
    return ((home // 2) * (blocks + 2) + wide) * 2 + home % 2


def local_entries(blocks):
    return [(a, b, REACH + b - a) for a in range(blocks) for b in range(a, blocks)]


def side_entries(blocks, after):
    if after:
        return [(a, b, 2 * REACH + b - a) for a in range(blocks) for b in range(a + 1)]
    return [(a, b, b - a) for a in range(blocks) for b in range(a, blocks)]


def list_side(blocks, after, pattern_ref, list_ref):
    count = jnp.int32(0)
    for home, other, column in side_entries(blocks, after):
        list_ref[count] = jnp.int32(entry(side_slot(blocks, home, other, after), 0, other, home))
        count = count + pattern_ref[home, column]
    return count


def pad_list(count, list_ref, spare):
    for k in range(TAIL - 1):
        list_ref[count + k] = jnp.int32(entry(spare, spare, 0, 0))


def clear_tiles(count, list_ref, tiles_ref):
    mask = (1 << FIELD) - 1

    def step(at, carry):
        code = list_ref[at]
        tiles_ref[code & mask] = jnp.zeros((BLK, BLK), bf16)
        tiles_ref[(code >> FIELD) & mask] = jnp.zeros((BLK, BLK), bf16)
        return carry

    lax.fori_loop(0, count, step, 0)


def products(vec, tiles_ref, pair, wide):
    tiles = tiles_ref[pair * 2 * wide : (pair + 1) * 2 * wide].reshape(wide, 2, BLK, BLK)
    tiles = jnp.concatenate([tiles[:, 0].reshape(wide * BLK, BLK), tiles[:, 1].reshape(wide * BLK, BLK)], axis=1)
    return jnp.dot(vec, tiles, preferred_element_type=f32)


def pair_cols(pair):
    return slice(pair * 2 * BLK, (pair + 1) * 2 * BLK)


def local_products(blocks, vec, tiles_ref, out_ref):
    for pair in range(blocks // 2):
        out_ref[:, pair_cols(pair)] = products(vec, tiles_ref, pair, blocks)


def gather_sides(blocks, before, side_a, side_b, wide_ref):
    size = blocks * BLK
    at_a = pl.multiple_of(jnp.where(before == 1, 0, size), size)
    at_b = pl.multiple_of(size - at_a, size)
    wide_ref[:, pl.ds(at_a, size)] = side_a
    wide_ref[:, pl.ds(at_b, size)] = side_b


def side_products(blocks, pair, wide_ref, tiles_ref):
    vec = wide_ref[:, pair * 2 * BLK : (pair * 2 + blocks + 2) * BLK]
    return products(vec, tiles_ref, pair, blocks + 2)


def prep_kernel(points_ref, vec_ref, out_ref):
    out_ref[:F, :] = points_ref[...]
    out_ref[F:, :] = vec_ref[...].astype(bf16)


def local_kernel(
    blocks, pattern_ref, own_ref, local_ref, side_ref, right_ref, part_ref, left_ref, list_ref, dead_ref
):
    spare = blocks * blocks
    fill_features(own_ref[:F, :], left_ref, right_ref)
    dead = jnp.int32(0)
    for after in (False, True):
        for home, other, column in side_entries(blocks, after):
            slot = side_slot(blocks, home, other, after)
            dead_ref[dead] = jnp.int32(entry(slot, slot, 0, 0))
            dead = dead + (1 - pattern_ref[home, column])
    clear_tiles(dead, dead_ref, side_ref)
    for pair in range(blocks // 2):
        first = pair * 2 * (blocks + 2)
        side_ref[first + 1] = jnp.zeros((BLK, BLK), bf16)
        side_ref[first + 2 * (blocks + 1)] = jnp.zeros((BLK, BLK), bf16)
    dead = jnp.int32(0)
    count = jnp.int32(0)
    for home, other, column in local_entries(blocks):
        code = jnp.int32(entry(local_slot(blocks, home, other), local_slot(blocks, other, home), other, home))
        live = pattern_ref[home, column]
        dead_ref[dead] = code
        list_ref[count] = code
        dead = dead + (1 - live)
        count = count + live
    pad_list(count, list_ref, spare)
    clear_tiles(dead, dead_ref, local_ref)
    make_tiles(count, list_ref, left_ref, right_ref, local_ref, True)
    local_products(blocks, own_ref[F:, :], local_ref, part_ref)


def make_side(blocks, before, pattern_ref, other_ref, right_ref, tiles_ref, left_ref, list_ref, count_ref):
    fill_features(other_ref[:F, :], left_ref, None)

    @pl.when(before == 1)
    def _():
        count_ref[0] = list_side(blocks, False, pattern_ref, list_ref)

    @pl.when(before == 0)
    def _():
        count_ref[0] = list_side(blocks, True, pattern_ref, list_ref)

    count = count_ref[0]
    pad_list(count, list_ref, blocks * (blocks + 2))
    make_tiles(count, list_ref, left_ref, right_ref, tiles_ref, False)


def side_kernel(blocks, before_ref, pattern_ref, other_ref, right_ref, tiles_in, tiles_ref, left_ref, list_ref, count_ref):
    del tiles_in
    make_side(blocks, before_ref[0], pattern_ref, other_ref, right_ref, tiles_ref, left_ref, list_ref, count_ref)


def first_kernel(
    blocks, before_ref, pattern_ref, a_ref, b_ref, right_ref, tiles_in, part_ref, noise_ref, vec_ref,
    tiles_ref, image_ref, low_ref, left_ref, wide_ref, list_ref, count_ref,
):
    del tiles_in
    before = before_ref[0]
    make_side(blocks, 1 - before, pattern_ref, b_ref, right_ref, tiles_ref, left_ref, list_ref, count_ref)
    gather_sides(blocks, before, a_ref[F:, :], b_ref[F:, :], wide_ref)
    for pair in range(blocks // 2):
        cols = pair_cols(pair)
        total = part_ref[:, cols] + side_products(blocks, pair, wide_ref, tiles_ref)
        image = noise_ref[:, cols] * vec_ref[:, cols] + total * SCALE
        image_ref[:, cols] = image
        low_ref[:, cols] = image.astype(bf16)


def own_kernel(blocks, own_ref, tiles_ref, part_ref):
    local_products(blocks, own_ref[:, : blocks * BLK], tiles_ref, part_ref)


def second_kernel(
    blocks, before_ref, a_ref, b_ref, tiles_ref, part_ref, noise_ref, vec_ref, image_ref,
    twice_ref, low_ref, sums_ref, wide_ref,
):
    width, points = vec_ref.shape
    gather_sides(blocks, before_ref[0], a_ref[...], b_ref[...], wide_ref)
    totals = [jnp.zeros((width, LANES), f32) for _ in range(SUMS)]
    for pair in range(blocks // 2):
        cols = pair_cols(pair)
        r = vec_ref[:, cols]
        w = image_ref[:, cols]
        q = noise_ref[:, cols] * w + (part_ref[:, cols] + side_products(blocks, pair, wide_ref, tiles_ref)) * SCALE
        twice_ref[:, cols] = q
        u = r - SHIFT * w
        y = w - SHIFT * q
        low_ref[:width, cols] = y.astype(bf16)
        low_ref[width:, cols] = q.astype(bf16)
        terms = (r * r, r * w, u * u, u * w, w * w, y * u, q * u, y * w, q * w)
        totals = [total + (term[:, :LANES] + term[:, LANES:]) for total, term in zip(totals, terms)]
    lane = lax.broadcasted_iota(jnp.int32, (width, LANES), 1)
    out = jnp.zeros((width, LANES), f32)
    for at, total in enumerate(totals):
        out = jnp.where(lane == at, jnp.sum(total, axis=1, keepdims=True), out)
    sums_ref[...] = out
    high, middle, low = three_parts(out)
    low_ref[:width, points : points + LANES] = high.astype(bf16)
    low_ref[:width, points + LANES :] = middle.astype(bf16)
    low_ref[width:, points : points + LANES] = low.astype(bf16)
    low_ref[width:, points + LANES :] = jnp.zeros((width, LANES), bf16)


def third_kernel(blocks, before_ref, a_ref, b_ref, tiles_ref, part_ref, out_ref, wide_ref):
    points = blocks * BLK
    gather_sides(blocks, before_ref[0], a_ref[:, :points], b_ref[:, :points], wide_ref)
    for pair in range(blocks // 2):
        cols = pair_cols(pair)
        out_ref[:, cols] = (part_ref[:, cols] + side_products(blocks, pair, wide_ref, tiles_ref)) * SCALE


def last_kernel(sums_ref, noise_ref, vec_ref, image_ref, twice_ref, prod_ref, x_ref, r_ref, w_ref):
    width = vec_ref.shape[0]
    rr, rw, uu, uw, ww, yu, qu, yw, qw = [sums_ref[:, at : at + 1] for at in range(SUMS)]
    alpha0 = rr / rw
    delta = alpha0 - SHIFT
    norm = uu - 2.0 * delta * uw + delta * delta * ww
    curv = yu - delta * (qu + yw) + delta * delta * qw
    beta = norm / rr
    alpha1 = norm / (curv - beta * norm / alpha0)
    r0, w0, q0 = vec_ref[...], image_ref[...], twice_ref[...]
    r1 = r0 - alpha0 * w0
    w1 = w0 - alpha0 * q0
    q1 = noise_ref[...] * w1 + (prod_ref[:width, :] - delta * prod_ref[width:, :])
    x_ref[...] = alpha0 * r0 + alpha1 * (r1 + beta * r0)
    r_ref[...] = r1 - alpha1 * (w1 + beta * w0)
    w_ref[...] = w1 - alpha1 * (q1 + beta * q0)


def swap_pairs(count, first):
    pairs = []
    for low in range(first, count - 1, 2):
        pairs += [(low, low + 1), (low + 1, low)]
    return pairs


def both_sides(x):
    count = lax.axis_size("pts")
    return (
        lax.ppermute(x, "pts", swap_pairs(count, 0)),
        lax.ppermute(x, "pts", swap_pairs(count, 1)),
    )


def total_over_points(own, neighbour, width):
    count = lax.axis_size("pts")
    if count & (count - 1):
        return lax.psum(own, "pts")
    if count == 1:
        return own
    parts = neighbour[:, -2 * LANES :].astype(f32)
    x = own + ((parts[:width, :LANES] + parts[:width, LANES:]) + parts[width:, :LANES])
    step = 2
    while step < count:
        reach = 4 if step * 2 < count else 2
        x = x + sum(
            lax.ppermute(x, "pts", [(i, i ^ (k * step)) for i in range(count)]) for k in range(1, reach)
        )
        step *= reach
    return x


def near(x):
    return pltpu.with_memory_space_constraint(x, pltpu.VMEM)


VM = pl.BlockSpec(memory_space=pltpu.VMEM)
SM = pl.BlockSpec(memory_space=pltpu.SMEM)


def per_device(points, noise_var, right_side, pattern):
    local_rows = points.shape[0]
    width = right_side.shape[0]
    blocks = local_rows // BLK
    assert blocks == REACH
    before = (lax.axis_index("pts") % 2).astype(jnp.int32).reshape(1)
    params = pltpu.CompilerParams(vmem_limit_bytes=20 * MIB)
    full = (width, local_rows)
    local_type = pltpu.VMEM((blocks * blocks + 1, BLK, BLK), bf16)
    side_type = pltpu.VMEM((blocks * (blocks + 2) + 1, BLK, BLK), bf16)
    left_scratch = pltpu.VMEM((blocks, BLK, LANES), bf16)
    list_scratch = pltpu.SMEM((blocks * (blocks + 1) // 2 + TAIL,), jnp.int32)
    count_scratch = pltpu.SMEM((1,), jnp.int32)
    dead_scratch = pltpu.SMEM((blocks * (blocks + 1) + 1,), jnp.int32)

    def wide(rows):
        return pltpu.VMEM((rows, 2 * local_rows), bf16)

    def call(kernel, name, ins, outs, scratch=(), aliases=None, scalars=0, us=2):
        return pl.pallas_call(
            kernel,
            out_shape=outs,
            in_specs=[SM] * scalars + [VM] * (len(ins) - scalars),
            out_specs=jax.tree.map(lambda _: VM, outs, is_leaf=lambda x: hasattr(x, "dtype")),
            scratch_shapes=list(scratch),
            input_output_aliases=aliases or {},
            compiler_params=params,
            cost_estimate=pl.CostEstimate(flops=us * 10**9, bytes_accessed=us * 3 * 10**6, transcendentals=0),
            name=name,
        )(*ins[:scalars], *[near(x) for x in ins[scalars:]])

    noise = noise_var[None, :]
    payload = call(
        prep_kernel, "prep", (points.T, right_side), pltpu.VMEM((F + width, local_rows), bf16)
    )
    halo_a, halo_b = both_sides(payload)
    local_tiles, side_tiles, right, part = call(
        functools.partial(local_kernel, blocks),
        "local_tiles",
        (pattern, payload),
        (local_type, side_type, pltpu.VMEM((blocks, LANES, BLK), bf16), pltpu.VMEM(full, f32)),
        (left_scratch, list_scratch, dead_scratch),
        scalars=1,
        us=8,
    )
    side_tiles = call(
        functools.partial(side_kernel, blocks),
        "side_tiles",
        (before, pattern, halo_a, right, side_tiles),
        side_type,
        (left_scratch, list_scratch, count_scratch),
        {4: 0},
        scalars=2,
        us=5,
    )
    side_tiles, image, low = call(
        functools.partial(first_kernel, blocks),
        "image",
        (before, pattern, halo_a, halo_b, right, side_tiles, part, noise, right_side),
        (side_type, pltpu.VMEM(full, f32), pltpu.VMEM(full, bf16)),
        (left_scratch, wide(width), list_scratch, count_scratch),
        {5: 0},
        scalars=2,
        us=7,
    )
    low_a, low_b = both_sides(low)
    part = call(
        functools.partial(own_kernel, blocks), "own_products", (low, local_tiles), pltpu.VMEM(full, f32)
    )
    low_type = pltpu.VMEM((2 * width, local_rows + 2 * LANES), bf16)
    twice, low, sums = call(
        functools.partial(second_kernel, blocks),
        "twice",
        (before, low_a, low_b, side_tiles, part, noise, right_side, image),
        (pltpu.VMEM(full, f32), low_type, pltpu.VMEM((width, LANES), f32)),
        (wide(width),),
        scalars=1,
    )
    low_a, low_b = both_sides(low)
    sums = total_over_points(sums, low_a, width)
    both = pltpu.VMEM((2 * width, local_rows), f32)
    part = call(functools.partial(own_kernel, blocks), "own_products_both", (low, local_tiles), both)
    prods = call(
        functools.partial(third_kernel, blocks),
        "products",
        (before, low_a, low_b, side_tiles, part),
        both,
        (wide(2 * width),),
        scalars=1,
    )
    out = jax.ShapeDtypeStruct(full, f32)
    return call(last_kernel, "update", (sums, noise, right_side, image, twice, prods), (out, out, out))


def solution(mesh):
    placed = (P("pts", None), P("pts"), P("rhs", "pts"), P("pts", None))
    return jax.shard_map(
        per_device,
        mesh=mesh,
        in_specs=placed,
        out_specs=(P("rhs", "pts"), P("rhs", "pts"), P("rhs", "pts")),
        check_vma=False,
    )
```

```python
import functools

import jax
import jax.numpy as jnp
from jax import lax
from jax.experimental import pallas as pl
from jax.experimental.pallas import tpu as pltpu
from jax.sharding import PartitionSpec as P

F = 32
BLK = 128
REACH = 16
WEXP = 18
LANES = 128
GAMMA = float(WEXP) ** (1.0 / (WEXP + 1))
GAMMA_SQ = GAMMA * GAMMA
OFFSET = GAMMA * (WEXP + 1) / WEXP
TINY = 1e-30
SCALE = 1.0 / (4 * BLK)
SHIFT = 2.0 / (0.5 + 0.6)
SUMS = 9
UNROLL = 16
TAIL = 4
FIELD = 10
MIB = 1 << 20

f32 = jnp.float32
bf16 = jnp.bfloat16


def rounded(x):
    return x.astype(bf16).astype(f32)


def three_parts(x):
    high = rounded(x)
    rest = x - high
    middle = rounded(rest)
    return high, middle, rounded(rest - middle)


def eight_rows(rows):
    row = lax.broadcasted_iota(jnp.int32, (8, rows[0].shape[1]), 0)
    out = jnp.zeros((8, rows[0].shape[1]), f32)
    for at, value in enumerate(rows):
        out = jnp.where(row == at, value, out)
    return out


def fill_features(points, left_ref, right_ref):
    x = points.astype(f32)
    count = x.shape[1]
    squares = three_parts(GAMMA_SQ * jnp.sum(x * x, axis=0, keepdims=True))
    ones = [jnp.ones((1, count), f32)] * 3
    blank = jnp.zeros((LANES - 3 * F - 8, count), f32)
    left = jnp.concatenate([x, x, x, eight_rows(list(squares) + ones), blank], axis=0).astype(bf16)
    for b in range(count // BLK):
        left_ref[b] = left[:, b * BLK : (b + 1) * BLK].T
    if right_ref is not None:
        cross = three_parts((-2.0 * GAMMA_SQ) * x)
        right = jnp.concatenate(list(cross) + [eight_rows(ones + list(squares)), blank], axis=0).astype(bf16)
        for b in range(count // BLK):
            right_ref[b] = right[:, b * BLK : (b + 1) * BLK]


def tile_values(left, right):
    scaled = jnp.dot(left, right, preferred_element_type=f32)
    scaled = jnp.maximum(scaled, TINY)
    s = jnp.maximum(GAMMA - scaled * lax.rsqrt(scaled), 0.0)
    s2 = s * s
    s4 = s2 * s2
    s8 = s4 * s4
    s16 = s8 * s8
    return ((s16 * s2) * (OFFSET - s)).astype(bf16)


def entry(slot, mirror, other, home):
    return (((((home << 4) + other) << FIELD) + mirror) << FIELD) + slot


def make_tiles(count, list_ref, left_ref, right_ref, tiles_ref, mirrored):
    mask = (1 << FIELD) - 1

    def one(at):
        code = list_ref[at]
        home = code >> (2 * FIELD + 4)
        other = (code >> (2 * FIELD)) & 15
        tile = tile_values(left_ref[other], right_ref[home])
        if mirrored:
            tiles_ref[(code >> FIELD) & mask] = tile.T
        tiles_ref[code & mask] = tile

    def step(at, carry):
        for k in range(UNROLL):
            one(at * UNROLL + k)
        return carry

    def tail(at, carry):
        for k in range(TAIL):
            one(at * TAIL + k)
        return carry

    whole = count // UNROLL
    lax.fori_loop(0, whole, step, 0)
    lax.fori_loop(whole * (UNROLL // TAIL), (count + TAIL - 1) // TAIL, tail, 0)


def local_slot(blocks, home, other):
    return ((home // 2) * blocks + other) * 2 + home % 2


def side_slot(blocks, home, other, after):
    wide = other - 2 * (home // 2) + (blocks if after else 0)
    return blocks * blocks + ((home // 2) * (blocks + 2) + wide) * 2 + home % 2


def spare_slot(blocks):
    return 2 * blocks * (blocks + 1)


def local_entries(blocks):
    return [(a, b, REACH + b - a) for a in range(blocks) for b in range(a, blocks)]


def side_entries(blocks, after):
    if after:
        return [(a, b, 2 * REACH + b - a) for a in range(blocks) for b in range(a + 1)]
    return [(a, b, b - a) for a in range(blocks) for b in range(a, blocks)]


def list_side(blocks, after, pattern_ref, list_ref):
    count = jnp.int32(0)
    for home, other, column in side_entries(blocks, after):
        list_ref[count] = jnp.int32(entry(side_slot(blocks, home, other, after), 0, other, home))
        count = count + pattern_ref[home, column]
    return count


def pad_list(count, list_ref, spare):
    for k in range(TAIL - 1):
        list_ref[count + k] = jnp.int32(entry(spare, spare, 0, 0))


def clear_tiles(count, list_ref, tiles_ref):
    mask = (1 << FIELD) - 1

    def step(at, carry):
        code = list_ref[at]
        tiles_ref[code & mask] = jnp.zeros((BLK, BLK), bf16)
        tiles_ref[(code >> FIELD) & mask] = jnp.zeros((BLK, BLK), bf16)
        return carry

    lax.fori_loop(0, count, step, 0)


def products(vec, tiles_ref, first, wide):
    tiles = tiles_ref[first : first + 2 * wide].reshape(wide, 2, BLK, BLK)
    tiles = jnp.concatenate([tiles[:, 0].reshape(wide * BLK, BLK), tiles[:, 1].reshape(wide * BLK, BLK)], axis=1)
    return jnp.dot(vec, tiles, preferred_element_type=f32)


def pair_cols(pair):
    return slice(pair * 2 * BLK, (pair + 1) * 2 * BLK)


def local_products(blocks, vec, tiles_ref, out_ref):
    for pair in range(blocks // 2):
        out_ref[:, pair_cols(pair)] = products(vec, tiles_ref, pair * 2 * blocks, blocks)


def gather_sides(blocks, before, side_a, side_b, wide_ref):
    size = blocks * BLK
    at_a = pl.multiple_of(jnp.where(before == 1, 0, size), size)
    at_b = pl.multiple_of(size - at_a, size)
    wide_ref[:, pl.ds(at_a, size)] = side_a
    wide_ref[:, pl.ds(at_b, size)] = side_b


def side_products(blocks, pair, wide_ref, tiles_ref):
    vec = wide_ref[:, pair * 2 * BLK : (pair * 2 + blocks + 2) * BLK]
    return products(vec, tiles_ref, blocks * blocks + pair * 2 * (blocks + 2), blocks + 2)


def prep_kernel(points_ref, vec_ref, out_ref):
    out_ref[:F, :] = points_ref[...]
    out_ref[F:, :] = vec_ref[...].astype(bf16)


def local_kernel(
    blocks, pattern_ref, own_ref, tiles_ref, right_ref, part_ref, left_ref, list_ref, dead_ref
):
    spare = spare_slot(blocks)
    fill_features(own_ref[:F, :], left_ref, right_ref)
    dead = jnp.int32(0)
    for after in (False, True):
        for home, other, column in side_entries(blocks, after):
            slot = side_slot(blocks, home, other, after)
            dead_ref[dead] = jnp.int32(entry(slot, slot, 0, 0))
            dead = dead + (1 - pattern_ref[home, column])
    clear_tiles(dead, dead_ref, tiles_ref)
    for pair in range(blocks // 2):
        first = blocks * blocks + pair * 2 * (blocks + 2)
        tiles_ref[first + 1] = jnp.zeros((BLK, BLK), bf16)
        tiles_ref[first + 2 * (blocks + 1)] = jnp.zeros((BLK, BLK), bf16)
    dead = jnp.int32(0)
    count = jnp.int32(0)
    for home, other, column in local_entries(blocks):
        code = jnp.int32(entry(local_slot(blocks, home, other), local_slot(blocks, other, home), other, home))
        live = pattern_ref[home, column]
        dead_ref[dead] = code
        list_ref[count] = code
        dead = dead + (1 - live)
        count = count + live
    pad_list(count, list_ref, spare)
    clear_tiles(dead, dead_ref, tiles_ref)
    make_tiles(count, list_ref, left_ref, right_ref, tiles_ref, True)
    local_products(blocks, own_ref[F:, :], tiles_ref, part_ref)


def make_side(blocks, before, pattern_ref, other_ref, right_ref, tiles_ref, left_ref, list_ref, count_ref):
    fill_features(other_ref[:F, :], left_ref, None)

    @pl.when(before == 1)
    def _():
        count_ref[0] = list_side(blocks, False, pattern_ref, list_ref)

    @pl.when(before == 0)
    def _():
        count_ref[0] = list_side(blocks, True, pattern_ref, list_ref)

    count = count_ref[0]
    pad_list(count, list_ref, spare_slot(blocks))
    make_tiles(count, list_ref, left_ref, right_ref, tiles_ref, False)


def side_kernel(blocks, before_ref, pattern_ref, other_ref, right_ref, tiles_in, tiles_ref, left_ref, list_ref, count_ref):
    del tiles_in
    make_side(blocks, before_ref[0], pattern_ref, other_ref, right_ref, tiles_ref, left_ref, list_ref, count_ref)


def first_kernel(
    blocks, before_ref, pattern_ref, a_ref, b_ref, right_ref, tiles_in, part_ref, noise_ref, vec_ref,
    tiles_ref, image_ref, low_ref, left_ref, wide_ref, list_ref, count_ref,
):
    del tiles_in
    before = before_ref[0]
    make_side(blocks, 1 - before, pattern_ref, b_ref, right_ref, tiles_ref, left_ref, list_ref, count_ref)
    gather_sides(blocks, before, a_ref[F:, :], b_ref[F:, :], wide_ref)
    for pair in range(blocks // 2):
        cols = pair_cols(pair)
        total = part_ref[:, cols] + side_products(blocks, pair, wide_ref, tiles_ref)
        image = noise_ref[:, cols] * vec_ref[:, cols] + total * SCALE
        image_ref[:, cols] = image
        low_ref[:, cols] = image.astype(bf16)


def own_kernel(blocks, own_ref, tiles_ref, part_ref):
    local_products(blocks, own_ref[:, : blocks * BLK], tiles_ref, part_ref)


def second_kernel(
    blocks, before_ref, a_ref, b_ref, tiles_ref, part_ref, noise_ref, vec_ref, image_ref,
    twice_ref, low_ref, sums_ref, wide_ref,
):
    width, points = vec_ref.shape
    gather_sides(blocks, before_ref[0], a_ref[...], b_ref[...], wide_ref)
    totals = [jnp.zeros((width, LANES), f32) for _ in range(SUMS)]
    for pair in range(blocks // 2):
        cols = pair_cols(pair)
        r = vec_ref[:, cols]
        w = image_ref[:, cols]
        q = noise_ref[:, cols] * w + (part_ref[:, cols] + side_products(blocks, pair, wide_ref, tiles_ref)) * SCALE
        twice_ref[:, cols] = q
        u = r - SHIFT * w
        y = w - SHIFT * q
        low_ref[:width, cols] = y.astype(bf16)
        low_ref[width:, cols] = q.astype(bf16)
        terms = (r * r, r * w, u * u, u * w, w * w, y * u, q * u, y * w, q * w)
        totals = [total + (term[:, :LANES] + term[:, LANES:]) for total, term in zip(totals, terms)]
    lane = lax.broadcasted_iota(jnp.int32, (width, LANES), 1)
    out = jnp.zeros((width, LANES), f32)
    for at, total in enumerate(totals):
        out = jnp.where(lane == at, jnp.sum(total, axis=1, keepdims=True), out)
    sums_ref[...] = out
    high, middle, low = three_parts(out)
    low_ref[:width, points : points + LANES] = high.astype(bf16)
    low_ref[:width, points + LANES :] = middle.astype(bf16)
    low_ref[width:, points : points + LANES] = low.astype(bf16)
    low_ref[width:, points + LANES :] = jnp.zeros((width, LANES), bf16)


def third_kernel(blocks, before_ref, a_ref, b_ref, tiles_ref, part_ref, out_ref, wide_ref):
    points = blocks * BLK
    gather_sides(blocks, before_ref[0], a_ref[:, :points], b_ref[:, :points], wide_ref)
    for pair in range(blocks // 2):
        cols = pair_cols(pair)
        out_ref[:, cols] = (part_ref[:, cols] + side_products(blocks, pair, wide_ref, tiles_ref)) * SCALE


def last_kernel(sums_ref, noise_ref, vec_ref, image_ref, twice_ref, prod_ref, x_ref, r_ref, w_ref):
    width = vec_ref.shape[0]
    rr, rw, uu, uw, ww, yu, qu, yw, qw = [sums_ref[:, at : at + 1] for at in range(SUMS)]
    alpha0 = rr / rw
    delta = alpha0 - SHIFT
    norm = uu - 2.0 * delta * uw + delta * delta * ww
    curv = yu - delta * (qu + yw) + delta * delta * qw
    beta = norm / rr
    alpha1 = norm / (curv - beta * norm / alpha0)
    r0, w0, q0 = vec_ref[...], image_ref[...], twice_ref[...]
    r1 = r0 - alpha0 * w0
    w1 = w0 - alpha0 * q0
    q1 = noise_ref[...] * w1 + (prod_ref[:width, :] - delta * prod_ref[width:, :])
    x_ref[...] = alpha0 * r0 + alpha1 * (r1 + beta * r0)
    r_ref[...] = r1 - alpha1 * (w1 + beta * w0)
    w_ref[...] = w1 - alpha1 * (q1 + beta * q0)


def swap_pairs(count, first):
    pairs = []
    for low in range(first, count - 1, 2):
        pairs += [(low, low + 1), (low + 1, low)]
    return pairs


def both_sides(x):
    count = lax.axis_size("pts")
    return (
        lax.ppermute(x, "pts", swap_pairs(count, 0)),
        lax.ppermute(x, "pts", swap_pairs(count, 1)),
    )


def total_over_points(own, neighbour, width):
    count = lax.axis_size("pts")
    if count & (count - 1):
        return lax.psum(own, "pts")
    if count == 1:
        return own
    parts = neighbour[:, -2 * LANES :].astype(f32)
    x = own + ((parts[:width, :LANES] + parts[:width, LANES:]) + parts[width:, :LANES])
    step = 2
    while step < count:
        reach = 4 if step * 2 < count else 2
        x = x + sum(
            lax.ppermute(x, "pts", [(i, i ^ (k * step)) for i in range(count)]) for k in range(1, reach)
        )
        step *= reach
    return x


def near(x):
    return pltpu.with_memory_space_constraint(x, pltpu.VMEM)


VM = pl.BlockSpec(memory_space=pltpu.VMEM)
SM = pl.BlockSpec(memory_space=pltpu.SMEM)


def per_device(points, noise_var, right_side, pattern):
    local_rows = points.shape[0]
    width = right_side.shape[0]
    blocks = local_rows // BLK
    assert blocks == REACH
    before = (lax.axis_index("pts") % 2).astype(jnp.int32).reshape(1)
    params = pltpu.CompilerParams(vmem_limit_bytes=12 * MIB)
    full = (width, local_rows)
    tiles_type = pltpu.VMEM((spare_slot(blocks) + 1, BLK, BLK), bf16)
    left_scratch = pltpu.VMEM((blocks, BLK, LANES), bf16)
    list_scratch = pltpu.SMEM((blocks * (blocks + 1) // 2 + TAIL,), jnp.int32)
    count_scratch = pltpu.SMEM((1,), jnp.int32)
    dead_scratch = pltpu.SMEM((blocks * (blocks + 1) + 1,), jnp.int32)

    def wide(rows):
        return pltpu.VMEM((rows, 2 * local_rows), bf16)

    def call(kernel, name, ins, outs, scratch=(), aliases=None, scalars=0, us=2):
        return pl.pallas_call(
            kernel,
            out_shape=outs,
            in_specs=[SM] * scalars + [VM] * (len(ins) - scalars),
            out_specs=jax.tree.map(lambda _: VM, outs, is_leaf=lambda x: hasattr(x, "dtype")),
            scratch_shapes=list(scratch),
            input_output_aliases=aliases or {},
            compiler_params=params,
            cost_estimate=pl.CostEstimate(flops=10**9, bytes_accessed=10**7, transcendentals=0),
            name=name,
        )(*ins[:scalars], *[near(x) for x in ins[scalars:]])

    noise = noise_var[None, :]
    payload = call(
        prep_kernel, "prep", (points.T, right_side), pltpu.VMEM((F + width, local_rows), bf16)
    )
    halo_a, halo_b = both_sides(payload)
    tiles, right, part = call(
        functools.partial(local_kernel, blocks),
        "local_tiles",
        (pattern, payload),
        (tiles_type, pltpu.VMEM((blocks, LANES, BLK), bf16), pltpu.VMEM(full, f32)),
        (left_scratch, list_scratch, dead_scratch),
        scalars=1,
        us=8,
    )
    tiles = call(
        functools.partial(side_kernel, blocks),
        "side_tiles",
        (before, pattern, halo_a, right, tiles),
        tiles_type,
        (left_scratch, list_scratch, count_scratch),
        {4: 0},
        scalars=2,
        us=5,
    )
    tiles, image, low = call(
        functools.partial(first_kernel, blocks),
        "image",
        (before, pattern, halo_a, halo_b, right, tiles, part, noise, right_side),
        (tiles_type, pltpu.VMEM(full, f32), pltpu.VMEM(full, bf16)),
        (left_scratch, wide(width), list_scratch, count_scratch),
        {5: 0},
        scalars=2,
        us=7,
    )
    low_a, low_b = both_sides(low)
    part = call(
        functools.partial(own_kernel, blocks), "own_products", (low, tiles), pltpu.VMEM(full, f32)
    )
    low_type = pltpu.VMEM((2 * width, local_rows + 2 * LANES), bf16)
    twice, low, sums = call(
        functools.partial(second_kernel, blocks),
        "twice",
        (before, low_a, low_b, tiles, part, noise, right_side, image),
        (pltpu.VMEM(full, f32), low_type, pltpu.VMEM((width, LANES), f32)),
        (wide(width),),
        scalars=1,
    )
    low_a, low_b = both_sides(low)
    sums = total_over_points(sums, low_a, width)
    both = pltpu.VMEM((2 * width, local_rows), f32)
    part = call(functools.partial(own_kernel, blocks), "own_products_both", (low, tiles), both)
    prods = call(
        functools.partial(third_kernel, blocks),
        "products",
        (before, low_a, low_b, tiles, part),
        both,
        (wide(2 * width),),
        scalars=1,
    )
    out = jax.ShapeDtypeStruct(full, f32)
    return call(last_kernel, "update", (sums, noise, right_side, image, twice, prods), (out, out, out))


def solution(mesh):
    placed = (P("pts", None), P("pts"), P("rhs", "pts"), P("pts", None))
    return jax.shard_map(
        per_device,
        mesh=mesh,
        in_specs=placed,
        out_specs=(P("rhs", "pts"), P("rhs", "pts"), P("rhs", "pts")),
        check_vma=False,
    )
```

```python
import functools

import jax
import jax.numpy as jnp
from jax import lax
from jax.experimental import pallas as pl
from jax.experimental.pallas import tpu as pltpu
from jax.sharding import PartitionSpec as P

F = 32
BLK = 128
REACH = 16
WEXP = 18
LANES = 128
GAMMA = float(WEXP) ** (1.0 / (WEXP + 1))
GAMMA_SQ = GAMMA * GAMMA
OFFSET = GAMMA * (WEXP + 1) / WEXP
TINY = 1e-30
SCALE = 1.0 / (4 * BLK)
SHIFT = 2.0 / (0.5 + 0.6)
SUMS = 9
STEPS = (32, 16, 8)
FIELD = 10
MIB = 1 << 20

f32 = jnp.float32
bf16 = jnp.bfloat16


def rounded(x):
    return x.astype(bf16).astype(f32)


def three_parts(x):
    high = rounded(x)
    rest = x - high
    middle = rounded(rest)
    return high, middle, rounded(rest - middle)


def eight_rows(rows):
    row = lax.broadcasted_iota(jnp.int32, (8, rows[0].shape[1]), 0)
    out = jnp.zeros((8, rows[0].shape[1]), f32)
    for at, value in enumerate(rows):
        out = jnp.where(row == at, value, out)
    return out


def fill_features(points, left_ref, first, right_ref=None):
    x = points.astype(f32)
    count = x.shape[1]
    squares = three_parts(GAMMA_SQ * jnp.sum(x * x, axis=0, keepdims=True))
    ones = [jnp.ones((1, count), f32)] * 3
    blank = jnp.zeros((LANES - 3 * F - 8, count), f32)
    left = jnp.concatenate([x, x, x, eight_rows(list(squares) + ones), blank], axis=0).astype(bf16)
    for b in range(count // BLK):
        left_ref[first + b] = left[:, b * BLK : (b + 1) * BLK].T
    if right_ref is not None:
        cross = three_parts((-2.0 * GAMMA_SQ) * x)
        right = jnp.concatenate(list(cross) + [eight_rows(ones + list(squares)), blank], axis=0).astype(bf16)
        for b in range(count // BLK):
            right_ref[b] = right[:, b * BLK : (b + 1) * BLK]


def tile_values(left, right):
    scaled = jnp.dot(left, right, preferred_element_type=f32)
    scaled = jnp.maximum(scaled, TINY)
    s = jnp.maximum(GAMMA - scaled * lax.rsqrt(scaled), 0.0)
    s2 = s * s
    s4 = s2 * s2
    s8 = s4 * s4
    s16 = s8 * s8
    return ((s16 * s2) * (OFFSET - s)).astype(bf16)


def entry(slot, mirror, other, home):
    return (((((home << 5) + other) << FIELD) + mirror) << FIELD) + slot


def make_tiles(count, list_ref, left_ref, right_ref, tiles_ref, mirrored):
    mask = (1 << FIELD) - 1

    def one(at):
        code = list_ref[at]
        home = code >> (2 * FIELD + 5)
        other = (code >> (2 * FIELD)) & 31
        tile = tile_values(left_ref[other], right_ref[home])
        if mirrored:
            tiles_ref[(code >> FIELD) & mask] = tile.T
        tiles_ref[code & mask] = tile

    done = jnp.int32(0)
    for size in STEPS:

        def step(at, carry, size=size, done=done):
            for k in range(size):
                one(done + at * size + k)
            return carry

        last = size == STEPS[-1]
        steps = (count - done + (size - 1 if last else 0)) // size
        lax.fori_loop(0, steps, step, 0)
        done = done + steps * size


def local_slot(blocks, home, other):
    return ((home // 2) * blocks + other) * 2 + home % 2


def side_slot(blocks, home, other, after):
    wide = other - 2 * (home // 2) + (blocks if after else 0)
    return blocks * blocks + ((home // 2) * (blocks + 2) + wide) * 2 + home % 2


def spare_slot(blocks):
    return 2 * blocks * (blocks + 1)


def local_entries(blocks):
    return [(a, b, REACH + b - a) for a in range(blocks) for b in range(a, blocks)]


def side_entries(blocks, after):
    if after:
        return [(a, b, 2 * REACH + b - a) for a in range(blocks) for b in range(a + 1)]
    return [(a, b, b - a) for a in range(blocks) for b in range(a, blocks)]


def pad_list(count, list_ref, spare):
    for k in range(STEPS[-1] - 1):
        list_ref[count + k] = jnp.int32(entry(spare, spare, 0, 0))


def clear_tiles(count, list_ref, tiles_ref):
    mask = (1 << FIELD) - 1

    def step(at, carry):
        code = list_ref[at]
        tiles_ref[code & mask] = jnp.zeros((BLK, BLK), bf16)
        tiles_ref[(code >> FIELD) & mask] = jnp.zeros((BLK, BLK), bf16)
        return carry

    lax.fori_loop(0, count, step, 0)


def products(vec, tiles_ref, first, wide):
    tiles = tiles_ref[first : first + 2 * wide].reshape(wide, 2, BLK, BLK)
    tiles = jnp.concatenate([tiles[:, 0].reshape(wide * BLK, BLK), tiles[:, 1].reshape(wide * BLK, BLK)], axis=1)
    return jnp.dot(vec, tiles, preferred_element_type=f32)


def pair_cols(pair):
    return slice(pair * 2 * BLK, (pair + 1) * 2 * BLK)


def local_products(blocks, vec, tiles_ref, out_ref):
    for pair in range(blocks // 2):
        out_ref[:, pair_cols(pair)] = products(vec, tiles_ref, pair * 2 * blocks, blocks)


def gather_sides(blocks, before, side_a, side_b, wide_ref):
    size = blocks * BLK
    at_a = pl.multiple_of(jnp.where(before == 1, 0, size), size)
    at_b = pl.multiple_of(size - at_a, size)
    wide_ref[:, pl.ds(at_a, size)] = side_a
    wide_ref[:, pl.ds(at_b, size)] = side_b


def side_products(blocks, pair, wide_ref, tiles_ref):
    vec = wide_ref[:, pair * 2 * BLK : (pair * 2 + blocks + 2) * BLK]
    return products(vec, tiles_ref, blocks * blocks + pair * 2 * (blocks + 2), blocks + 2)


def odd_place():
    return lax.rem(lax.axis_index("pts"), 2)


def prep_kernel(points_ref, vec_ref, out_ref, wide_ref, sems):
    points_copy = pltpu.make_async_copy(points_ref, out_ref.at[:F], sems.at[0])
    vec_copy = pltpu.make_async_copy(vec_ref, wide_ref, sems.at[1])
    vec_copy.start()
    points_copy.start()
    vec_copy.wait()
    out_ref[F:, :] = wide_ref[...].astype(bf16)
    points_copy.wait()


def local_kernel(
    blocks, pattern_ref, own_ref, tiles_ref, right_ref, part_ref, left_ref, listed_ref, list_ref, dead_ref, sem
):
    pattern_copy = pltpu.make_async_copy(pattern_ref, listed_ref, sem)
    pattern_copy.start()
    fill_features(own_ref[:F, :], left_ref, 0, right_ref)
    first = blocks * blocks
    for pair in range(blocks // 2):

        def clear(at, carry, start=first + pair * 2 * (blocks + 2)):
            tiles_ref[pl.ds(start + at * 4, 4)] = jnp.zeros((4, BLK, BLK), bf16)
            return carry

        lax.fori_loop(0, (blocks + 2) // 2, clear, 0)
    pattern_copy.wait()
    dead = jnp.int32(0)
    count = jnp.int32(0)
    for home, other, column in local_entries(blocks):
        code = jnp.int32(entry(local_slot(blocks, home, other), local_slot(blocks, other, home), other, home))
        live = listed_ref[home, column]
        dead_ref[dead] = code
        list_ref[count] = code
        dead = dead + (1 - live)
        count = count + live
    pad_list(count, list_ref, spare_slot(blocks))
    clear_tiles(dead, dead_ref, tiles_ref)
    make_tiles(count, list_ref, left_ref, right_ref, tiles_ref, True)
    local_products(blocks, own_ref[F:, :], tiles_ref, part_ref)


def first_kernel(
    blocks, pattern_ref, a_ref, b_ref, right_ref, tiles_in, part_ref, noise_ref, vec_ref,
    tiles_ref, image_ref, low_ref, left_ref, wide_ref, listed_ref, list_ref, sem,
):
    del tiles_in
    pattern_copy = pltpu.make_async_copy(pattern_ref, listed_ref, sem)
    pattern_copy.start()
    before = odd_place()
    fill_features(a_ref[:F, :], left_ref, (1 - before) * blocks)
    fill_features(b_ref[:F, :], left_ref, before * blocks)
    gather_sides(blocks, before, a_ref[F:, :], b_ref[F:, :], wide_ref)
    pattern_copy.wait()
    count = jnp.int32(0)
    for after in (False, True):
        for home, other, column in side_entries(blocks, after):
            slot = side_slot(blocks, home, other, after)
            list_ref[count] = jnp.int32(entry(slot, 0, other + (blocks if after else 0), home))
            count = count + listed_ref[home, column]
    pad_list(count, list_ref, spare_slot(blocks))
    make_tiles(count, list_ref, left_ref, right_ref, tiles_ref, False)
    for pair in range(blocks // 2):
        cols = pair_cols(pair)
        total = part_ref[:, cols] + side_products(blocks, pair, wide_ref, tiles_ref)
        image = noise_ref[:, cols] * vec_ref[:, cols] + total * SCALE
        image_ref[:, cols] = image
        low_ref[:, cols] = image.astype(bf16)


def own_kernel(blocks, own_ref, tiles_ref, part_ref):
    local_products(blocks, own_ref[...], tiles_ref, part_ref)


def second_kernel(
    blocks, a_ref, b_ref, tiles_ref, part_ref, noise_ref, vec_ref, image_ref,
    twice_ref, low_ref, sums_ref, wide_ref,
):
    width = vec_ref.shape[0]
    gather_sides(blocks, odd_place(), a_ref[...], b_ref[...], wide_ref)
    totals = [jnp.zeros((width, LANES), f32) for _ in range(SUMS)]
    for pair in range(blocks // 2):
        cols = pair_cols(pair)
        r = vec_ref[:, cols]
        w = image_ref[:, cols]
        q = noise_ref[:, cols] * w + (part_ref[:, cols] + side_products(blocks, pair, wide_ref, tiles_ref)) * SCALE
        twice_ref[:, cols] = q
        u = r - SHIFT * w
        y = w - SHIFT * q
        low_ref[:width, cols] = y.astype(bf16)
        low_ref[width:, cols] = q.astype(bf16)
        terms = (r * r, r * w, u * u, u * w, w * w, y * u, q * u, y * w, q * w)
        totals = [total + (term[:, :LANES] + term[:, LANES:]) for total, term in zip(totals, terms)]
    lane = lax.broadcasted_iota(jnp.int32, (width, LANES), 1)
    out = jnp.zeros((width, LANES), f32)
    for at, total in enumerate(totals):
        out = jnp.where(lane == at, jnp.sum(total, axis=1, keepdims=True), out)
    sums_ref[...] = out


def third_kernel(blocks, a_ref, b_ref, tiles_ref, part_ref, out_ref, wide_ref):
    gather_sides(blocks, odd_place(), a_ref[...], b_ref[...], wide_ref)
    for pair in range(blocks // 2):
        cols = pair_cols(pair)
        out_ref[:, cols] = (part_ref[:, cols] + side_products(blocks, pair, wide_ref, tiles_ref)) * SCALE


def last_kernel(sums_ref, noise_ref, vec_ref, image_ref, twice_ref, prod_ref, x_ref, r_ref, w_ref):
    width = vec_ref.shape[0]
    rr, rw, uu, uw, ww, yu, qu, yw, qw = [sums_ref[:, at : at + 1] for at in range(SUMS)]
    alpha0 = rr / rw
    delta = alpha0 - SHIFT
    norm = uu - 2.0 * delta * uw + delta * delta * ww
    curv = yu - delta * (qu + yw) + delta * delta * qw
    beta = norm / rr
    alpha1 = norm / (curv - beta * norm / alpha0)
    r0, w0, q0 = vec_ref[...], image_ref[...], twice_ref[...]
    r1 = r0 - alpha0 * w0
    w1 = w0 - alpha0 * q0
    q1 = noise_ref[...] * w1 + (prod_ref[:width, :] - delta * prod_ref[width:, :])
    x_ref[...] = alpha0 * r0 + alpha1 * (r1 + beta * r0)
    r_ref[...] = r1 - alpha1 * (w1 + beta * w0)
    w_ref[...] = w1 - alpha1 * (q1 + beta * q0)


def swap_pairs(count, first):
    pairs = []
    for low in range(first, count - 1, 2):
        pairs += [(low, low + 1), (low + 1, low)]
    return pairs


def both_sides(x):
    count = lax.axis_size("pts")
    return (
        lax.ppermute(x, "pts", swap_pairs(count, 0)),
        lax.ppermute(x, "pts", swap_pairs(count, 1)),
    )


def total_over_points(x):
    count = lax.axis_size("pts")
    if count & (count - 1):
        return lax.psum(x, "pts")
    step = count
    while step > 1:
        size = 4 if step > 4 else 2
        step //= size
        x = x + sum(
            lax.ppermute(x, "pts", [(i, i ^ (k * step)) for i in range(count)]) for k in range(1, size)
        )
    return x


VM = pl.BlockSpec(memory_space=pltpu.VMEM)
FAR = pl.BlockSpec(memory_space=pltpu.HBM)


def per_device(points, noise_var, right_side, pattern):
    local_rows = points.shape[0]
    width = right_side.shape[0]
    blocks = local_rows // BLK
    assert blocks == REACH
    params = pltpu.CompilerParams(vmem_limit_bytes=12 * MIB)
    full = (width, local_rows)
    tiles_type = pltpu.VMEM((spare_slot(blocks) + 1, BLK, BLK), bf16)
    pairs = blocks * (blocks + 1) // 2
    listed = pltpu.SMEM(pattern.shape, jnp.int32)
    copied = pltpu.SemaphoreType.DMA(())

    def left(count):
        return pltpu.VMEM((count * blocks, BLK, LANES), bf16)

    def numbers(count):
        return pltpu.SMEM((count + STEPS[-1],), jnp.int32)

    def wide(rows):
        return pltpu.VMEM((rows, 2 * local_rows), bf16)

    def call(kernel, name, ins, outs, scratch=(), aliases=None, far=0):
        return pl.pallas_call(
            kernel,
            out_shape=outs,
            in_specs=[FAR] * far + [VM] * (len(ins) - far),
            out_specs=jax.tree.map(lambda _: VM, outs, is_leaf=lambda x: hasattr(x, "dtype")),
            scratch_shapes=list(scratch),
            input_output_aliases=aliases or {},
            compiler_params=params,
            cost_estimate=pl.CostEstimate(flops=10**9, bytes_accessed=10**7, transcendentals=0),
            name=name,
        )(*[pltpu.with_memory_space_constraint(x, pltpu.HBM) for x in ins[:far]], *[pltpu.with_memory_space_constraint(x, pltpu.VMEM) for x in ins[far:]])

    noise = noise_var[None, :]
    payload = call(
        prep_kernel,
        "prep",
        (points.T, right_side),
        pltpu.VMEM((F + width, local_rows), bf16),
        (pltpu.VMEM(full, f32), pltpu.SemaphoreType.DMA((2,))),
        far=2,
    )
    halo_a, halo_b = both_sides(payload)
    tiles, right, part = call(
        functools.partial(local_kernel, blocks),
        "local_tiles",
        (pattern, payload),
        (tiles_type, pltpu.VMEM((blocks, LANES, BLK), bf16), pltpu.VMEM(full, f32)),
        (left(1), listed, numbers(pairs), numbers(pairs), copied),
        far=1,
    )
    tiles, image, low = call(
        functools.partial(first_kernel, blocks),
        "image",
        (pattern, halo_a, halo_b, right, tiles, part, noise, right_side),
        (tiles_type, pltpu.VMEM(full, f32), pltpu.VMEM(full, bf16)),
        (left(2), wide(width), listed, numbers(2 * pairs), copied),
        {4: 0},
        far=1,
    )
    low_a, low_b = both_sides(low)
    part = call(
        functools.partial(own_kernel, blocks), "own_products", (low, tiles), pltpu.VMEM(full, f32)
    )
    twice, low, sums = call(
        functools.partial(second_kernel, blocks),
        "twice",
        (low_a, low_b, tiles, part, noise, right_side, image),
        (
            pltpu.VMEM(full, f32),
            pltpu.VMEM((2 * width, local_rows), bf16),
            pltpu.VMEM((width, LANES), f32),
        ),
        (wide(width),),
    )
    low_a, low_b = both_sides(low)
    sums = total_over_points(sums)
    both = pltpu.VMEM((2 * width, local_rows), f32)
    part = call(functools.partial(own_kernel, blocks), "own_products_both", (low, tiles), both)
    prods = call(
        functools.partial(third_kernel, blocks),
        "products",
        (low_a, low_b, tiles, part),
        both,
        (wide(2 * width),),
    )
    out = jax.ShapeDtypeStruct(full, f32)
    return call(last_kernel, "update", (sums, noise, right_side, image, twice, prods), (out, out, out))


def solution(mesh):
    placed = (P("pts", None), P("pts"), P("rhs", "pts"), P("pts", None))
    return jax.shard_map(
        per_device,
        mesh=mesh,
        in_specs=placed,
        out_specs=(P("rhs", "pts"), P("rhs", "pts"), P("rhs", "pts")),
        check_vma=False,
    )
```

```python
import functools

import jax
import jax.numpy as jnp
from jax import lax
from jax.experimental import pallas as pl
from jax.experimental.pallas import tpu as pltpu
from jax.sharding import PartitionSpec as P

F = 32
BLK = 128
REACH = 16
WEXP = 18
LANES = 128
GAMMA = float(WEXP) ** (1.0 / (WEXP + 1))
GAMMA_SQ = GAMMA * GAMMA
OFFSET = GAMMA * (WEXP + 1) / WEXP
TINY = 1e-30
SCALE = 1.0 / (4 * BLK)
SHIFT = 2.0 / (0.5 + 0.6)
SUMS = 9
STEPS = (32, 16, 8)
FIELD = 10
MIB = 1 << 20

f32 = jnp.float32
bf16 = jnp.bfloat16


def rounded(x):
    return x.astype(bf16).astype(f32)


def three_parts(x):
    high = rounded(x)
    rest = x - high
    middle = rounded(rest)
    return high, middle, rounded(rest - middle)


def eight_rows(rows):
    row = lax.broadcasted_iota(jnp.int32, (8, rows[0].shape[1]), 0)
    out = jnp.zeros((8, rows[0].shape[1]), f32)
    for at, value in enumerate(rows):
        out = jnp.where(row == at, value, out)
    return out


def fill_features(points, left_ref, first, right_ref=None):
    x = points.astype(f32)
    count = x.shape[1]
    squares = three_parts(GAMMA_SQ * jnp.sum(x * x, axis=0, keepdims=True))
    ones = [jnp.ones((1, count), f32)] * 3
    blank = jnp.zeros((LANES - 3 * F - 8, count), f32)
    left = jnp.concatenate([x, x, x, eight_rows(list(squares) + ones), blank], axis=0).astype(bf16)
    for b in range(count // BLK):
        left_ref[first + b] = left[:, b * BLK : (b + 1) * BLK].T
    if right_ref is not None:
        cross = three_parts((-2.0 * GAMMA_SQ) * x)
        right = jnp.concatenate(list(cross) + [eight_rows(ones + list(squares)), blank], axis=0).astype(bf16)
        for b in range(count // BLK):
            right_ref[b] = right[:, b * BLK : (b + 1) * BLK]


def tile_values(left, right):
    scaled = jnp.dot(left, right, preferred_element_type=f32)
    scaled = jnp.maximum(scaled, TINY)
    s = jnp.maximum(GAMMA - scaled * lax.rsqrt(scaled), 0.0)
    s2 = s * s
    s4 = s2 * s2
    s8 = s4 * s4
    s16 = s8 * s8
    return ((s16 * s2) * (OFFSET - s)).astype(bf16)


def entry(slot, mirror, other, home):
    return (((((home << 5) + other) << FIELD) + mirror) << FIELD) + slot


def make_tiles(count, list_ref, left_ref, right_ref, tiles_ref, mirrored):
    mask = (1 << FIELD) - 1

    def one(at):
        code = list_ref[at]
        home = code >> (2 * FIELD + 5)
        other = (code >> (2 * FIELD)) & 31
        tile = tile_values(left_ref[other], right_ref[home])
        if mirrored:
            tiles_ref[(code >> FIELD) & mask] = tile.T
        tiles_ref[code & mask] = tile

    done = jnp.int32(0)
    for size in STEPS:

        def step(at, carry, size=size, done=done):
            for k in range(size):
                one(done + at * size + k)
            return carry

        last = size == STEPS[-1]
        steps = (count - done + (size - 1 if last else 0)) // size
        lax.fori_loop(0, steps, step, 0)
        done = done + steps * size


def local_slot(blocks, home, other):
    return ((home // 2) * blocks + other) * 2 + home % 2


def side_slot(blocks, home, other, after):
    wide = other - 2 * (home // 2) + (blocks if after else 0)
    return blocks * blocks + ((home // 2) * (blocks + 2) + wide) * 2 + home % 2


def spare_slot(blocks):
    return 2 * blocks * (blocks + 1)


def local_entries(blocks):
    return [(a, b, REACH + b - a) for a in range(blocks) for b in range(a, blocks)]


def side_entries(blocks, after):
    if after:
        return [(a, b, 2 * REACH + b - a) for a in range(blocks) for b in range(a + 1)]
    return [(a, b, b - a) for a in range(blocks) for b in range(a, blocks)]


def pad_list(count, list_ref, spare):
    for k in range(STEPS[-1] - 1):
        list_ref[count + k] = jnp.int32(entry(spare, spare, 0, 0))


def clear_tiles(count, list_ref, tiles_ref):
    mask = (1 << FIELD) - 1

    def step(at, carry):
        code = list_ref[at]
        tiles_ref[code & mask] = jnp.zeros((BLK, BLK), bf16)
        tiles_ref[(code >> FIELD) & mask] = jnp.zeros((BLK, BLK), bf16)
        return carry

    lax.fori_loop(0, count, step, 0)


def products(vec, tiles_ref, first, wide):
    tiles = tiles_ref[first : first + 2 * wide].reshape(wide, 2, BLK, BLK)
    tiles = jnp.concatenate([tiles[:, 0].reshape(wide * BLK, BLK), tiles[:, 1].reshape(wide * BLK, BLK)], axis=1)
    return jnp.dot(vec, tiles, preferred_element_type=f32)


def pair_cols(pair):
    return slice(pair * 2 * BLK, (pair + 1) * 2 * BLK)


def local_products(blocks, vec, tiles_ref, out_ref):
    for pair in range(blocks // 2):
        out_ref[:, pair_cols(pair)] = products(vec, tiles_ref, pair * 2 * blocks, blocks)


def gather_sides(blocks, before, side_a, side_b, wide_ref):
    size = blocks * BLK
    at_a = pl.multiple_of(jnp.where(before == 1, 0, size), size)
    at_b = pl.multiple_of(size - at_a, size)
    wide_ref[:, pl.ds(at_a, size)] = side_a
    wide_ref[:, pl.ds(at_b, size)] = side_b


def side_products(blocks, pair, wide_ref, tiles_ref):
    vec = wide_ref[:, pair * 2 * BLK : (pair * 2 + blocks + 2) * BLK]
    return products(vec, tiles_ref, blocks * blocks + pair * 2 * (blocks + 2), blocks + 2)


def odd_place():
    return lax.rem(lax.axis_index("pts"), 2)


def prep_kernel(points_ref, vec_ref, noise_ref, out_ref, near_vec_ref, near_noise_ref, sems):
    points_copy = pltpu.make_async_copy(points_ref, out_ref.at[:F], sems.at[0])
    vec_copy = pltpu.make_async_copy(vec_ref, near_vec_ref, sems.at[1])
    noise_copy = pltpu.make_async_copy(noise_ref, near_noise_ref, sems.at[2])
    vec_copy.start()
    points_copy.start()
    noise_copy.start()
    vec_copy.wait()
    out_ref[F:, :] = near_vec_ref[...].astype(bf16)
    points_copy.wait()
    noise_copy.wait()


def local_kernel(
    blocks, pattern_ref, own_ref, tiles_ref, right_ref, part_ref, left_ref, listed_ref, list_ref, dead_ref, sem
):
    pattern_copy = pltpu.make_async_copy(pattern_ref, listed_ref, sem)
    pattern_copy.start()
    fill_features(own_ref[:F, :], left_ref, 0, right_ref)
    first = blocks * blocks
    for pair in range(blocks // 2):

        def clear(at, carry, start=first + pair * 2 * (blocks + 2)):
            tiles_ref[pl.ds(start + at * 4, 4)] = jnp.zeros((4, BLK, BLK), bf16)
            return carry

        lax.fori_loop(0, (blocks + 2) // 2, clear, 0)
    pattern_copy.wait()
    dead = jnp.int32(0)
    count = jnp.int32(0)
    for home, other, column in local_entries(blocks):
        code = jnp.int32(entry(local_slot(blocks, home, other), local_slot(blocks, other, home), other, home))
        live = listed_ref[home, column]
        dead_ref[dead] = code
        list_ref[count] = code
        dead = dead + (1 - live)
        count = count + live
    pad_list(count, list_ref, spare_slot(blocks))
    clear_tiles(dead, dead_ref, tiles_ref)
    make_tiles(count, list_ref, left_ref, right_ref, tiles_ref, True)
    local_products(blocks, own_ref[F:, :], tiles_ref, part_ref)


def first_kernel(
    blocks, pattern_ref, a_ref, b_ref, right_ref, tiles_in, part_ref, noise_ref, vec_ref,
    tiles_ref, image_ref, low_ref, left_ref, wide_ref, listed_ref, list_ref, sem,
):
    del tiles_in
    pattern_copy = pltpu.make_async_copy(pattern_ref, listed_ref, sem)
    pattern_copy.start()
    before = odd_place()
    fill_features(a_ref[:F, :], left_ref, (1 - before) * blocks)
    fill_features(b_ref[:F, :], left_ref, before * blocks)
    gather_sides(blocks, before, a_ref[F:, :], b_ref[F:, :], wide_ref)
    pattern_copy.wait()
    count = jnp.int32(0)
    for after in (False, True):
        for home, other, column in side_entries(blocks, after):
            slot = side_slot(blocks, home, other, after)
            list_ref[count] = jnp.int32(entry(slot, 0, other + (blocks if after else 0), home))
            count = count + listed_ref[home, column]
    pad_list(count, list_ref, spare_slot(blocks))
    make_tiles(count, list_ref, left_ref, right_ref, tiles_ref, False)
    for pair in range(blocks // 2):
        cols = pair_cols(pair)
        total = part_ref[:, cols] + side_products(blocks, pair, wide_ref, tiles_ref)
        image = noise_ref[:, cols] * vec_ref[:, cols] + total * SCALE
        image_ref[:, cols] = image
        low_ref[:, cols] = image.astype(bf16)


def own_kernel(blocks, own_ref, tiles_ref, part_ref):
    local_products(blocks, own_ref[:, : blocks * BLK], tiles_ref, part_ref)


def second_kernel(
    blocks, a_ref, b_ref, tiles_ref, part_ref, noise_ref, vec_ref, image_ref,
    twice_ref, low_ref, sums_ref, wide_ref,
):
    width = vec_ref.shape[0]
    gather_sides(blocks, odd_place(), a_ref[...], b_ref[...], wide_ref)
    totals = [jnp.zeros((width, LANES), f32) for _ in range(SUMS)]
    for pair in range(blocks // 2):
        cols = pair_cols(pair)
        r = vec_ref[:, cols]
        w = image_ref[:, cols]
        q = noise_ref[:, cols] * w + (part_ref[:, cols] + side_products(blocks, pair, wide_ref, tiles_ref)) * SCALE
        twice_ref[:, cols] = q
        u = r - SHIFT * w
        y = w - SHIFT * q
        low_ref[:, cols] = y.astype(bf16)
        terms = (r * r, r * w, u * u, u * w, w * w, y * u, q * u, y * w, q * w)
        totals = [total + (term[:, :LANES] + term[:, LANES:]) for total, term in zip(totals, terms)]
    lane = lax.broadcasted_iota(jnp.int32, (width, LANES), 1)
    out = jnp.zeros((width, LANES), f32)
    for at, total in enumerate(totals):
        out = jnp.where(lane == at, jnp.sum(total, axis=1, keepdims=True), out)
    sums_ref[...] = out
    points = blocks * BLK
    for at, part in enumerate(three_parts(out)):
        low_ref[:, points + at * LANES : points + (at + 1) * LANES] = part.astype(bf16)


def third_kernel(blocks, a_ref, b_ref, tiles_ref, part_ref, out_ref, wide_ref):
    points = blocks * BLK
    gather_sides(blocks, odd_place(), a_ref[:, :points], b_ref[:, :points], wide_ref)
    for pair in range(blocks // 2):
        cols = pair_cols(pair)
        out_ref[:, cols] = (part_ref[:, cols] + side_products(blocks, pair, wide_ref, tiles_ref)) * SCALE


def last_kernel(sums_ref, noise_ref, vec_ref, image_ref, twice_ref, prod_ref, x_ref, r_ref, w_ref):
    rr, rw, uu, uw, ww, yu, qu, yw, qw = [sums_ref[:, at : at + 1] for at in range(SUMS)]
    alpha0 = rr / rw
    delta = alpha0 - SHIFT
    norm = uu - 2.0 * delta * uw + delta * delta * ww
    curv = yu - delta * (qu + yw) + delta * delta * qw
    beta = norm / rr
    alpha1 = norm / (curv - beta * norm / alpha0)
    r0, w0, q0 = vec_ref[...], image_ref[...], twice_ref[...]
    r1 = r0 - alpha0 * w0
    w1 = w0 - alpha0 * q0
    share = alpha0 * (1.0 / SHIFT)
    q1 = noise_ref[...] * w1 + (1.0 - share) * (q0 - noise_ref[...] * w0) + share * prod_ref[...]
    x_ref[...] = alpha0 * r0 + alpha1 * (r1 + beta * r0)
    r_ref[...] = r1 - alpha1 * (w1 + beta * w0)
    w_ref[...] = w1 - alpha1 * (q1 + beta * q0)


def swap_pairs(count, first):
    pairs = []
    for low in range(first, count - 1, 2):
        pairs += [(low, low + 1), (low + 1, low)]
    return pairs


def both_sides(x):
    count = lax.axis_size("pts")
    b = lax.ppermute(x, "pts", swap_pairs(count, 1))
    a = lax.ppermute(x, "pts", swap_pairs(count, 0))
    return a, b


def total_over_points(x, neighbour):
    count = lax.axis_size("pts")
    if count & (count - 1):
        return lax.psum(x, "pts")
    if count == 1:
        return x
    high, middle, low = [
        neighbour[:, neighbour.shape[1] - (3 - k) * LANES :][:, :LANES].astype(f32) for k in range(3)
    ]
    x = x + ((high + middle) + low)
    step = count
    while step > 2:
        size = 4 if step > 4 else 2
        step //= size
        x = x + sum(
            lax.ppermute(x, "pts", [(i, i ^ (k * step)) for i in range(count)]) for k in range(1, size)
        )
    return x


VM = pl.BlockSpec(memory_space=pltpu.VMEM)
FAR = pl.BlockSpec(memory_space=pltpu.HBM)


def per_device(points, noise_var, right_side, pattern):
    local_rows = points.shape[0]
    width = right_side.shape[0]
    blocks = local_rows // BLK
    assert blocks == REACH
    params = pltpu.CompilerParams(vmem_limit_bytes=12 * MIB)
    full = (width, local_rows)
    tiles_type = pltpu.VMEM((spare_slot(blocks) + 1, BLK, BLK), bf16)
    pairs = blocks * (blocks + 1) // 2
    listed = pltpu.SMEM(pattern.shape, jnp.int32)
    copied = pltpu.SemaphoreType.DMA(())

    def left(count):
        return pltpu.VMEM((count * blocks, BLK, LANES), bf16)

    def numbers(count):
        return pltpu.SMEM((count + STEPS[-1],), jnp.int32)

    def wide(rows):
        return pltpu.VMEM((rows, 2 * local_rows), bf16)

    def call(kernel, name, ins, outs, scratch=(), aliases=None, far=0):
        return pl.pallas_call(
            kernel,
            out_shape=outs,
            in_specs=[FAR] * far + [VM] * (len(ins) - far),
            out_specs=jax.tree.map(lambda _: VM, outs, is_leaf=lambda x: hasattr(x, "dtype")),
            scratch_shapes=list(scratch),
            input_output_aliases=aliases or {},
            compiler_params=params,
            cost_estimate=pl.CostEstimate(flops=10**9, bytes_accessed=10**7, transcendentals=0),
            name=name,
        )(*[pltpu.with_memory_space_constraint(x, pltpu.HBM) for x in ins[:far]], *[pltpu.with_memory_space_constraint(x, pltpu.VMEM) for x in ins[far:]])

    payload, vec, noise = call(
        prep_kernel,
        "prep",
        (points.T, right_side, noise_var[None, :]),
        (pltpu.VMEM((F + width, local_rows), bf16), pltpu.VMEM(full, f32), pltpu.VMEM((1, local_rows), f32)),
        (pltpu.SemaphoreType.DMA((3,)),),
        far=3,
    )
    halo_a, halo_b = both_sides(payload)
    tiles, right, part = call(
        functools.partial(local_kernel, blocks),
        "local_tiles",
        (pattern, payload),
        (tiles_type, pltpu.VMEM((blocks, LANES, BLK), bf16), pltpu.VMEM(full, f32)),
        (left(1), listed, numbers(pairs), numbers(pairs), copied),
        far=1,
    )
    tiles, image, low = call(
        functools.partial(first_kernel, blocks),
        "image",
        (pattern, halo_a, halo_b, right, tiles, part, noise, vec),
        (tiles_type, pltpu.VMEM(full, f32), pltpu.VMEM(full, bf16)),
        (left(2), wide(width), listed, numbers(2 * pairs), copied),
        {4: 0},
        far=1,
    )
    low_a, low_b = both_sides(low)
    part = call(
        functools.partial(own_kernel, blocks), "own_products", (low, tiles), pltpu.VMEM(full, f32)
    )
    twice, low, sums = call(
        functools.partial(second_kernel, blocks),
        "twice",
        (low_a, low_b, tiles, part, noise, vec, image),
        (
            pltpu.VMEM(full, f32),
            pltpu.VMEM((width, local_rows + 3 * LANES), bf16),
            pltpu.VMEM((width, LANES), f32),
        ),
        (wide(width),),
    )
    low_a, low_b = both_sides(low)
    sums = total_over_points(sums, low_a)
    part = call(functools.partial(own_kernel, blocks), "own_products_last", (low, tiles), pltpu.VMEM(full, f32))
    prods = call(
        functools.partial(third_kernel, blocks),
        "products",
        (low_a, low_b, tiles, part),
        pltpu.VMEM(full, f32),
        (wide(width),),
    )
    out = jax.ShapeDtypeStruct(full, f32)
    return call(last_kernel, "update", (sums, noise, vec, image, twice, prods), (out, out, out))


def solution(mesh):
    placed = (P("pts", None), P("pts"), P("rhs", "pts"), P("pts", None))
    return jax.shard_map(
        per_device,
        mesh=mesh,
        in_specs=placed,
        out_specs=(P("rhs", "pts"), P("rhs", "pts"), P("rhs", "pts")),
        check_vma=False,
    )
```

```python
import functools

import jax
import jax.numpy as jnp
from jax import lax
from jax.experimental import pallas as pl
from jax.experimental.pallas import tpu as pltpu
from jax.sharding import PartitionSpec as P

F = 32
BLK = 128
REACH = 16
WEXP = 18
LANES = 128
GAMMA = float(WEXP) ** (1.0 / (WEXP + 1))
GAMMA_SQ = GAMMA * GAMMA
OFFSET = GAMMA * (WEXP + 1) / WEXP
TINY = 1e-30
SCALE = 1.0 / (4 * BLK)
SHIFT = 2.0 / (0.5 + 0.6)
SUMS = 9
STEPS = (32, 16, 8)
FIELD = 10
MIB = 1 << 20

f32 = jnp.float32
bf16 = jnp.bfloat16


def rounded(x):
    return x.astype(bf16).astype(f32)


def three_parts(x):
    high = rounded(x)
    rest = x - high
    middle = rounded(rest)
    return high, middle, rounded(rest - middle)


def eight_rows(rows):
    row = lax.broadcasted_iota(jnp.int32, (8, rows[0].shape[1]), 0)
    out = jnp.zeros((8, rows[0].shape[1]), f32)
    for at, value in enumerate(rows):
        out = jnp.where(row == at, value, out)
    return out


def fill_features(points, left_ref, first, right_ref=None):
    x = points.astype(f32)
    count = x.shape[1]
    squares = three_parts(GAMMA_SQ * jnp.sum(x * x, axis=0, keepdims=True))
    ones = [jnp.ones((1, count), f32)] * 3
    blank = jnp.zeros((LANES - 3 * F - 8, count), f32)
    left = jnp.concatenate([x, x, x, eight_rows(list(squares) + ones), blank], axis=0).astype(bf16)
    for b in range(count // BLK):
        left_ref[first + b] = left[:, b * BLK : (b + 1) * BLK].T
    if right_ref is not None:
        cross = three_parts((-2.0 * GAMMA_SQ) * x)
        right = jnp.concatenate(list(cross) + [eight_rows(ones + list(squares)), blank], axis=0).astype(bf16)
        for b in range(count // BLK):
            right_ref[b] = right[:, b * BLK : (b + 1) * BLK]


def tile_values(left, right):
    scaled = jnp.dot(left, right, preferred_element_type=f32)
    scaled = jnp.maximum(scaled, TINY)
    s = jnp.maximum(GAMMA - scaled * lax.rsqrt(scaled), 0.0)
    s2 = s * s
    s4 = s2 * s2
    s8 = s4 * s4
    s16 = s8 * s8
    return ((s16 * s2) * (OFFSET - s)).astype(bf16)


def entry(slot, mirror, other, home):
    return (((((home << 5) + other) << FIELD) + mirror) << FIELD) + slot


def make_tiles(count, list_ref, left_ref, right_ref, tiles_ref, mirrored):
    mask = (1 << FIELD) - 1

    def one(at):
        code = list_ref[at]
        home = code >> (2 * FIELD + 5)
        other = (code >> (2 * FIELD)) & 31
        tile = tile_values(left_ref[other], right_ref[home])
        if mirrored:
            tiles_ref[(code >> FIELD) & mask] = tile.T
        tiles_ref[code & mask] = tile

    done = jnp.int32(0)
    for size in STEPS:

        def step(at, carry, size=size, done=done):
            for k in range(size):
                one(done + at * size + k)
            return carry

        last = size == STEPS[-1]
        steps = (count - done + (size - 1 if last else 0)) // size
        lax.fori_loop(0, steps, step, 0)
        done = done + steps * size


def local_slot(blocks, home, other):
    return ((home // 2) * blocks + other) * 2 + home % 2


def side_slot(blocks, home, other, after):
    wide = other - 2 * (home // 2) + (blocks if after else 0)
    return blocks * blocks + ((home // 2) * (blocks + 2) + wide) * 2 + home % 2


def spare_slot(blocks):
    return 2 * blocks * (blocks + 1)


def local_entries(blocks):
    return [(a, b, REACH + b - a) for a in range(blocks) for b in range(a, blocks)]


def side_entries(blocks, after):
    if after:
        return [(a, b, 2 * REACH + b - a) for a in range(blocks) for b in range(a + 1)]
    return [(a, b, b - a) for a in range(blocks) for b in range(a, blocks)]


def pad_list(count, list_ref, spare):
    for k in range(STEPS[-1] - 1):
        list_ref[count + k] = jnp.int32(entry(spare, spare, 0, 0))


def clear_tiles(count, list_ref, tiles_ref):
    mask = (1 << FIELD) - 1

    def step(at, carry):
        code = list_ref[at]
        tiles_ref[code & mask] = jnp.zeros((BLK, BLK), bf16)
        tiles_ref[(code >> FIELD) & mask] = jnp.zeros((BLK, BLK), bf16)
        return carry

    lax.fori_loop(0, count, step, 0)


def products(vec, tiles_ref, first, wide):
    tiles = tiles_ref[first : first + 2 * wide].reshape(wide, 2, BLK, BLK)
    tiles = jnp.concatenate([tiles[:, 0].reshape(wide * BLK, BLK), tiles[:, 1].reshape(wide * BLK, BLK)], axis=1)
    return jnp.dot(vec, tiles, preferred_element_type=f32)


def pair_cols(pair):
    return slice(pair * 2 * BLK, (pair + 1) * 2 * BLK)


def local_products(blocks, vec, tiles_ref, out_ref):
    for pair in range(blocks // 2):
        out_ref[:, pair_cols(pair)] = products(vec, tiles_ref, pair * 2 * blocks, blocks)


def gather_sides(blocks, before, side_a, side_b, wide_ref):
    size = blocks * BLK
    at_a = pl.multiple_of(jnp.where(before == 1, 0, size), size)
    at_b = pl.multiple_of(size - at_a, size)
    wide_ref[:, pl.ds(at_a, size)] = side_a
    wide_ref[:, pl.ds(at_b, size)] = side_b


def side_products(blocks, pair, wide_ref, tiles_ref):
    vec = wide_ref[:, pair * 2 * BLK : (pair * 2 + blocks + 2) * BLK]
    return products(vec, tiles_ref, blocks * blocks + pair * 2 * (blocks + 2), blocks + 2)


def odd_place():
    return lax.rem(lax.axis_index("pts"), 2)


def prep_kernel(points_ref, vec_ref, noise_ref, pattern_ref, out_ref, near_vec_ref, near_noise_ref, listed_ref, sems):
    points_copy = pltpu.make_async_copy(points_ref, out_ref.at[:F], sems.at[0])
    vec_copy = pltpu.make_async_copy(vec_ref, near_vec_ref, sems.at[1])
    noise_copy = pltpu.make_async_copy(noise_ref, near_noise_ref, sems.at[2])
    vec_copy.start()
    points_copy.start()
    noise_copy.start()
    pattern_copy = pltpu.make_async_copy(pattern_ref, listed_ref, sems.at[3])
    pattern_copy.start()
    vec_copy.wait()
    out_ref[F:, :] = near_vec_ref[...].astype(bf16)
    points_copy.wait()
    noise_copy.wait()
    pattern_copy.wait()


def local_kernel(blocks, listed_ref, own_ref, tiles_ref, right_ref, part_ref, left_ref, list_ref, dead_ref):
    fill_features(own_ref[:F, :], left_ref, 0, right_ref)
    for pair in range(blocks // 2):
        first = blocks * blocks + pair * 2 * (blocks + 2)
        tiles_ref[first + 1] = jnp.zeros((BLK, BLK), bf16)
        tiles_ref[first + 2 * (blocks + 1)] = jnp.zeros((BLK, BLK), bf16)
    entries = [
        (entry(local_slot(blocks, home, other), local_slot(blocks, other, home), other, home), home, column)
        for home, other, column in local_entries(blocks)
    ]
    count, dead = scan_entries(entries, listed_ref, list_ref, dead_ref)
    pad_list(count, list_ref, spare_slot(blocks))
    clear_tiles(dead, dead_ref, tiles_ref)
    make_tiles(count, list_ref, left_ref, right_ref, tiles_ref, True)
    local_products(blocks, own_ref[F:, :], tiles_ref, part_ref)


def scan_entries(entries, listed_ref, list_ref, dead_ref):
    count = jnp.int32(0)
    dead = jnp.int32(0)
    for code, home, column in entries:
        live = listed_ref[home, column]
        list_ref[count] = jnp.int32(code)
        dead_ref[dead] = jnp.int32(code)
        count = count + live
        dead = dead + (1 - live)
    return count, dead


def make_side(blocks, before, listed_ref, points, right_ref, tiles_ref, left_ref, list_ref, dead_ref, count_ref):
    fill_features(points, left_ref, 0)
    for after in (False, True):

        @pl.when(before == (0 if after else 1))
        def _(after=after):
            entries = []
            for home, other, column in side_entries(blocks, after):
                slot = side_slot(blocks, home, other, after)
                entries.append((entry(slot, slot, other, home), home, column))
            count, dead = scan_entries(entries, listed_ref, list_ref, dead_ref)
            count_ref[0] = count
            count_ref[1] = dead

    count = count_ref[0]
    pad_list(count, list_ref, spare_slot(blocks))
    clear_tiles(count_ref[1], dead_ref, tiles_ref)
    make_tiles(count, list_ref, left_ref, right_ref, tiles_ref, False)


def side_kernel(
    blocks, listed_ref, b_ref, right_ref, tiles_in, tiles_ref, left_ref, list_ref, dead_ref, count_ref
):
    del tiles_in
    make_side(
        blocks, 1 - odd_place(), listed_ref, b_ref[:F, :], right_ref, tiles_ref, left_ref, list_ref, dead_ref, count_ref
    )


def first_kernel(
    blocks, listed_ref, a_ref, b_ref, right_ref, tiles_in, part_ref, noise_ref, vec_ref,
    tiles_ref, image_ref, low_ref, left_ref, list_ref, dead_ref, count_ref, wide_ref,
):
    del tiles_in
    before = odd_place()
    make_side(
        blocks, before, listed_ref, a_ref[:F, :], right_ref, tiles_ref, left_ref, list_ref, dead_ref, count_ref
    )
    gather_sides(blocks, before, a_ref[F:, :], b_ref[F:, :], wide_ref)
    for pair in range(blocks // 2):
        cols = pair_cols(pair)
        total = part_ref[:, cols] + side_products(blocks, pair, wide_ref, tiles_ref)
        image = noise_ref[:, cols] * vec_ref[:, cols] + total * SCALE
        image_ref[:, cols] = image
        low_ref[:, cols] = image.astype(bf16)


def own_kernel(blocks, own_ref, tiles_ref, part_ref):
    local_products(blocks, own_ref[:, : blocks * BLK], tiles_ref, part_ref)


def second_kernel(
    blocks, a_ref, b_ref, tiles_ref, part_ref, noise_ref, vec_ref, image_ref,
    twice_ref, low_ref, sums_ref, wide_ref,
):
    width = vec_ref.shape[0]
    gather_sides(blocks, odd_place(), a_ref[...], b_ref[...], wide_ref)
    totals = [jnp.zeros((width, LANES), f32) for _ in range(SUMS)]
    for pair in range(blocks // 2):
        cols = pair_cols(pair)
        r = vec_ref[:, cols]
        w = image_ref[:, cols]
        q = noise_ref[:, cols] * w + (part_ref[:, cols] + side_products(blocks, pair, wide_ref, tiles_ref)) * SCALE
        twice_ref[:, cols] = q
        u = r - SHIFT * w
        y = w - SHIFT * q
        low_ref[:, cols] = y.astype(bf16)
        terms = (r * r, r * w, u * u, u * w, w * w, y * u, q * u, y * w, q * w)
        totals = [total + (term[:, :LANES] + term[:, LANES:]) for total, term in zip(totals, terms)]
    lane = lax.broadcasted_iota(jnp.int32, (width, LANES), 1)
    out = jnp.zeros((width, LANES), f32)
    for at, total in enumerate(totals):
        out = jnp.where(lane == at, jnp.sum(total, axis=1, keepdims=True), out)
    sums_ref[...] = out
    points = blocks * BLK
    for at, part in enumerate(three_parts(out)):
        low_ref[:, points + at * LANES : points + (at + 1) * LANES] = part.astype(bf16)


def third_kernel(blocks, a_ref, b_ref, tiles_ref, part_ref, out_ref, wide_ref):
    points = blocks * BLK
    gather_sides(blocks, odd_place(), a_ref[:, :points], b_ref[:, :points], wide_ref)
    for pair in range(blocks // 2):
        cols = pair_cols(pair)
        out_ref[:, cols] = (part_ref[:, cols] + side_products(blocks, pair, wide_ref, tiles_ref)) * SCALE


def last_kernel(sums_ref, noise_ref, vec_ref, image_ref, twice_ref, prod_ref, x_ref, r_ref, w_ref):
    rr, rw, uu, uw, ww, yu, qu, yw, qw = [sums_ref[:, at : at + 1] for at in range(SUMS)]
    alpha0 = rr / rw
    delta = alpha0 - SHIFT
    norm = uu - 2.0 * delta * uw + delta * delta * ww
    curv = yu - delta * (qu + yw) + delta * delta * qw
    beta = norm / rr
    alpha1 = norm / (curv - beta * norm / alpha0)
    r0, w0, q0 = vec_ref[...], image_ref[...], twice_ref[...]
    r1 = r0 - alpha0 * w0
    w1 = w0 - alpha0 * q0
    share = alpha0 * (1.0 / SHIFT)
    q1 = noise_ref[...] * w1 + (1.0 - share) * (q0 - noise_ref[...] * w0) + share * prod_ref[...]
    x_ref[...] = alpha0 * r0 + alpha1 * (r1 + beta * r0)
    r_ref[...] = r1 - alpha1 * (w1 + beta * w0)
    w_ref[...] = w1 - alpha1 * (q1 + beta * q0)


def swap_pairs(count, first):
    pairs = []
    for low in range(first, count - 1, 2):
        pairs += [(low, low + 1), (low + 1, low)]
    return pairs


def first_side(x):
    return lax.ppermute(x, "pts", swap_pairs(lax.axis_size("pts"), 0))


def second_side(x):
    return lax.ppermute(x, "pts", swap_pairs(lax.axis_size("pts"), 1))


def both_sides(x):
    return first_side(x), second_side(x)


def total_over_points(x, neighbour):
    count = lax.axis_size("pts")
    if count & (count - 1):
        return lax.psum(x, "pts")
    if count == 1:
        return x
    high, middle, low = [
        neighbour[:, neighbour.shape[1] - (3 - k) * LANES :][:, :LANES].astype(f32) for k in range(3)
    ]
    x = x + ((high + middle) + low)
    step = count
    while step > 2:
        size = 4 if step > 4 else 2
        step //= size
        x = x + sum(
            lax.ppermute(x, "pts", [(i, i ^ (k * step)) for i in range(count)]) for k in range(1, size)
        )
    return x


VM = pl.BlockSpec(memory_space=pltpu.VMEM)
FAR = pl.BlockSpec(memory_space=pltpu.HBM)
SM = pl.BlockSpec(memory_space=pltpu.SMEM)


def per_device(points, noise_var, right_side, pattern):
    local_rows = points.shape[0]
    width = right_side.shape[0]
    blocks = local_rows // BLK
    assert blocks == REACH
    params = pltpu.CompilerParams(vmem_limit_bytes=12 * MIB)
    full = (width, local_rows)
    tiles_type = pltpu.VMEM((spare_slot(blocks) + 1, BLK, BLK), bf16)
    pairs = blocks * (blocks + 1) // 2

    def numbers(count):
        return pltpu.SMEM((count,), jnp.int32)

    lists = (
        pltpu.VMEM((blocks, BLK, LANES), bf16),
        numbers(pairs + STEPS[-1]),
        numbers(pairs + 1),
    )
    wide = pltpu.VMEM((width, 2 * local_rows), bf16)

    def call(kernel, name, ins, outs, scratch=(), aliases=None, spaces=()):
        spaces = tuple(spaces) + (VM,) * (len(ins) - len(spaces))
        return pl.pallas_call(
            kernel,
            out_shape=outs,
            in_specs=list(spaces),
            out_specs=jax.tree.map(
                lambda x: SM if x.dtype == jnp.int32 else VM, outs, is_leaf=lambda x: hasattr(x, "dtype")
            ),
            scratch_shapes=list(scratch),
            input_output_aliases=aliases or {},
            compiler_params=params,
            cost_estimate=pl.CostEstimate(flops=10**9, bytes_accessed=10**7, transcendentals=0),
            name=name,
        )(*[pltpu.with_memory_space_constraint(x, space.memory_space) for x, space in zip(ins, spaces)])

    payload, vec, noise, listed = call(
        prep_kernel,
        "prep",
        (points.T, right_side, noise_var[None, :], pattern),
        (
            pltpu.VMEM((F + width, local_rows), bf16),
            pltpu.VMEM(full, f32),
            pltpu.VMEM((1, local_rows), f32),
            pltpu.SMEM(pattern.shape, jnp.int32),
        ),
        (pltpu.SemaphoreType.DMA((4,)),),
        spaces=(FAR,) * 4,
    )
    halo_a, halo_b = both_sides(payload)
    tiles, right, part = call(
        functools.partial(local_kernel, blocks),
        "local_tiles",
        (listed, payload),
        (tiles_type, pltpu.VMEM((blocks, LANES, BLK), bf16), pltpu.VMEM(full, f32)),
        lists,
        spaces=(SM,),
    )
    tiles = call(
        functools.partial(side_kernel, blocks),
        "side_tiles",
        (listed, halo_b, right, tiles),
        tiles_type,
        lists + (numbers(2),),
        {3: 0},
        spaces=(SM,),
    )
    tiles, image, low = call(
        functools.partial(first_kernel, blocks),
        "image",
        (listed, halo_a, halo_b, right, tiles, part, noise, vec),
        (tiles_type, pltpu.VMEM(full, f32), pltpu.VMEM(full, bf16)),
        lists + (numbers(2), wide),
        {4: 0},
        spaces=(SM,),
    )
    low_a, low_b = both_sides(low)
    part = call(
        functools.partial(own_kernel, blocks), "own_products", (low, tiles), pltpu.VMEM(full, f32)
    )
    twice, low, sums = call(
        functools.partial(second_kernel, blocks),
        "twice",
        (low_a, low_b, tiles, part, noise, vec, image),
        (
            pltpu.VMEM(full, f32),
            pltpu.VMEM((width, local_rows + 3 * LANES), bf16),
            pltpu.VMEM((width, LANES), f32),
        ),
        (wide,),
    )
    low_a = first_side(low)
    part = call(functools.partial(own_kernel, blocks), "own_products_last", (low, tiles), pltpu.VMEM(full, f32))
    low, part = lax.optimization_barrier((low, part))
    low_b = second_side(low)
    sums = total_over_points(sums, low_a)
    prods = call(
        functools.partial(third_kernel, blocks),
        "products",
        (low_a, low_b, tiles, part),
        pltpu.VMEM(full, f32),
        (wide,),
    )
    out = jax.ShapeDtypeStruct(full, f32)
    return call(last_kernel, "update", (sums, noise, vec, image, twice, prods), (out, out, out))


def solution(mesh):
    placed = (P("pts", None), P("pts"), P("rhs", "pts"), P("pts", None))
    return jax.shard_map(
        per_device,
        mesh=mesh,
        in_specs=placed,
        out_specs=(P("rhs", "pts"), P("rhs", "pts"), P("rhs", "pts")),
        check_vma=False,
    )
```

```python
import functools

import jax
import jax.numpy as jnp
from jax import lax
from jax.experimental import pallas as pl
from jax.experimental.pallas import tpu as pltpu
from jax.sharding import PartitionSpec as P

F = 32
BLK = 128
REACH = 16
WEXP = 18
LANES = 128
GAMMA = float(WEXP) ** (1.0 / (WEXP + 1))
GAMMA_SQ = GAMMA * GAMMA
OFFSET = GAMMA * (WEXP + 1) / WEXP
TINY = 1e-30
SCALE = 1.0 / (4 * BLK)
SHIFT = 2.0 / (0.5 + 0.6)
SUMS = 9
STEPS = (48, 16, 8)
FIELD = 10
MIB = 1 << 20

f32 = jnp.float32
bf16 = jnp.bfloat16


def rounded(x):
    return x.astype(bf16).astype(f32)


def three_parts(x):
    high = rounded(x)
    rest = x - high
    middle = rounded(rest)
    return high, middle, rounded(rest - middle)


def eight_rows(rows):
    row = lax.broadcasted_iota(jnp.int32, (8, rows[0].shape[1]), 0)
    out = jnp.zeros((8, rows[0].shape[1]), f32)
    for at, value in enumerate(rows):
        out = jnp.where(row == at, value, out)
    return out


def fill_features(points, left_ref, first, right_ref=None):
    x = points.astype(f32)
    count = x.shape[1]
    squares = three_parts(GAMMA_SQ * jnp.sum(x * x, axis=0, keepdims=True))
    ones = [jnp.ones((1, count), f32)] * 3
    blank = jnp.zeros((LANES - 3 * F - 8, count), f32)
    left = jnp.concatenate([x, x, x, eight_rows(list(squares) + ones), blank], axis=0).astype(bf16)
    for b in range(count // BLK):
        left_ref[first + b] = left[:, b * BLK : (b + 1) * BLK].T
    if right_ref is not None:
        cross = three_parts((-2.0 * GAMMA_SQ) * x)
        right = jnp.concatenate(list(cross) + [eight_rows(ones + list(squares)), blank], axis=0).astype(bf16)
        for b in range(count // BLK):
            right_ref[b] = right[:, b * BLK : (b + 1) * BLK]


def tile_values(left, right):
    scaled = jnp.dot(left, right, preferred_element_type=f32)
    scaled = jnp.maximum(scaled, TINY)
    s = jnp.maximum(GAMMA - scaled * lax.rsqrt(scaled), 0.0)
    s2 = s * s
    s4 = s2 * s2
    s8 = s4 * s4
    s16 = s8 * s8
    return ((s16 * s2) * (OFFSET - s)).astype(bf16)


def entry(slot, mirror, other, home):
    return (((((home << 5) + other) << FIELD) + mirror) << FIELD) + slot


def make_tiles(count, list_ref, left_ref, right_ref, tiles_ref, mirrored):
    mask = (1 << FIELD) - 1

    def one(at):
        code = list_ref[at]
        home = code >> (2 * FIELD + 5)
        other = (code >> (2 * FIELD)) & 31
        tile = tile_values(left_ref[other], right_ref[home])
        if mirrored:
            tiles_ref[(code >> FIELD) & mask] = tile.T
        tiles_ref[code & mask] = tile

    done = jnp.int32(0)
    for size in STEPS:

        def step(at, carry, size=size, done=done):
            for k in range(size):
                one(done + at * size + k)
            return carry

        last = size == STEPS[-1]
        steps = (count - done + (size - 1 if last else 0)) // size
        lax.fori_loop(0, steps, step, 0)
        done = done + steps * size


def local_slot(blocks, home, other):
    return ((home // 2) * blocks + other) * 2 + home % 2


def side_slot(blocks, home, other, after):
    wide = other - 2 * (home // 2) + (blocks if after else 0)
    return blocks * blocks + ((home // 2) * (blocks + 2) + wide) * 2 + home % 2


def spare_slot(blocks):
    return 2 * blocks * (blocks + 1)


def local_entries(blocks):
    return [(a, b, REACH + b - a) for a in range(blocks) for b in range(a, blocks)]


def side_entries(blocks, after):
    if after:
        return [(a, b, 2 * REACH + b - a) for a in range(blocks) for b in range(a + 1)]
    return [(a, b, b - a) for a in range(blocks) for b in range(a, blocks)]


def pad_list(count, list_ref, spare):
    for k in range(STEPS[-1] - 1):
        list_ref[count + k] = jnp.int32(entry(spare, spare, 0, 0))


def clear_tiles(first, last, list_ref, tiles_ref, mirrored):
    mask = (1 << FIELD) - 1

    def step(at, carry):
        code = list_ref[at]
        tiles_ref[code & mask] = jnp.zeros((BLK, BLK), bf16)
        if mirrored:
            tiles_ref[(code >> FIELD) & mask] = jnp.zeros((BLK, BLK), bf16)
        return carry

    lax.fori_loop(first, last, step, 0)


def products(vec, tiles_ref, first, wide):
    tiles = tiles_ref[first : first + 2 * wide].reshape(wide, 2, BLK, BLK)
    tiles = jnp.concatenate([tiles[:, 0].reshape(wide * BLK, BLK), tiles[:, 1].reshape(wide * BLK, BLK)], axis=1)
    return jnp.dot(vec, tiles, preferred_element_type=f32)


def pair_cols(pair):
    return slice(pair * 2 * BLK, (pair + 1) * 2 * BLK)


def local_products(blocks, vec, tiles_ref, out_ref):
    for pair in range(blocks // 2):
        out_ref[:, pair_cols(pair)] = products(vec, tiles_ref, pair * 2 * blocks, blocks)


def gather_sides(blocks, before, side_a, side_b, wide_ref):
    size = blocks * BLK
    at_a = pl.multiple_of(jnp.where(before == 1, 0, size), size)
    at_b = pl.multiple_of(size - at_a, size)
    wide_ref[:, pl.ds(at_a, size)] = side_a
    wide_ref[:, pl.ds(at_b, size)] = side_b


def side_products(blocks, pair, wide_ref, tiles_ref):
    vec = wide_ref[:, pair * 2 * BLK : (pair * 2 + blocks + 2) * BLK]
    return products(vec, tiles_ref, blocks * blocks + pair * 2 * (blocks + 2), blocks + 2)


def odd_place():
    return lax.rem(lax.axis_index("pts"), 2)


def prep_kernel(points_ref, vec_ref, noise_ref, pattern_ref, out_ref, near_vec_ref, near_noise_ref, listed_ref, sems):
    points_copy = pltpu.make_async_copy(points_ref, out_ref.at[:F], sems.at[0])
    vec_copy = pltpu.make_async_copy(vec_ref, near_vec_ref, sems.at[1])
    noise_copy = pltpu.make_async_copy(noise_ref, near_noise_ref, sems.at[2])
    vec_copy.start()
    points_copy.start()
    noise_copy.start()
    pattern_copy = pltpu.make_async_copy(pattern_ref, listed_ref, sems.at[3])
    pattern_copy.start()
    vec_copy.wait()
    out_ref[F:, :] = near_vec_ref[...].astype(bf16)
    points_copy.wait()
    noise_copy.wait()
    pattern_copy.wait()


def local_kernel(blocks, listed_ref, own_ref, tiles_ref, right_ref, part_ref, left_ref, list_ref):
    fill_features(own_ref[:F, :], left_ref, 0, right_ref)
    for pair in range(blocks // 2):
        first = blocks * blocks + pair * 2 * (blocks + 2)
        tiles_ref[first + 1] = jnp.zeros((BLK, BLK), bf16)
        tiles_ref[first + 2 * (blocks + 1)] = jnp.zeros((BLK, BLK), bf16)
    entries = [
        (entry(local_slot(blocks, home, other), local_slot(blocks, other, home), other, home), home, column)
        for home, other, column in local_entries(blocks)
    ]
    count = scan_entries(entries, listed_ref, list_ref)
    clear_tiles(count + STEPS[-1], list_ref.shape[0], list_ref, tiles_ref, True)
    pad_list(count, list_ref, spare_slot(blocks))
    make_tiles(count, list_ref, left_ref, right_ref, tiles_ref, True)
    local_products(blocks, own_ref[F:, :], tiles_ref, part_ref)


def scan_entries(entries, listed_ref, list_ref):
    size = list_ref.shape[0]
    count = jnp.int32(0)
    for at, (code, home, column) in enumerate(entries):
        live = listed_ref[home, column]
        list_ref[jnp.where(live == 1, count, size - 1 - at + count)] = jnp.int32(code)
        count = count + live
    return count


def make_side(blocks, before, listed_ref, points, right_ref, tiles_ref, left_ref, list_ref, count_ref):
    fill_features(points, left_ref, 0)
    for after in (False, True):

        @pl.when(before == (0 if after else 1))
        def _(after=after):
            entries = []
            for home, other, column in side_entries(blocks, after):
                slot = side_slot(blocks, home, other, after)
                entries.append((entry(slot, slot, other, home), home, column))
            count_ref[0] = scan_entries(entries, listed_ref, list_ref)

    count = count_ref[0]
    clear_tiles(count + STEPS[-1], list_ref.shape[0], list_ref, tiles_ref, False)
    pad_list(count, list_ref, spare_slot(blocks))
    make_tiles(count, list_ref, left_ref, right_ref, tiles_ref, False)


def side_kernel(
    blocks, listed_ref, b_ref, right_ref, tiles_in, tiles_ref, left_ref, list_ref, count_ref
):
    del tiles_in
    make_side(
        blocks, 1 - odd_place(), listed_ref, b_ref[:F, :], right_ref, tiles_ref, left_ref, list_ref, count_ref
    )


def first_kernel(
    blocks, listed_ref, a_ref, b_ref, right_ref, tiles_in, part_ref, noise_ref, vec_ref,
    tiles_ref, image_ref, low_ref, left_ref, list_ref, count_ref, wide_ref,
):
    del tiles_in
    before = odd_place()
    make_side(
        blocks, before, listed_ref, a_ref[:F, :], right_ref, tiles_ref, left_ref, list_ref, count_ref
    )
    gather_sides(blocks, before, a_ref[F:, :], b_ref[F:, :], wide_ref)
    for pair in range(blocks // 2):
        cols = pair_cols(pair)
        total = part_ref[:, cols] + side_products(blocks, pair, wide_ref, tiles_ref)
        image = noise_ref[:, cols] * vec_ref[:, cols] + total * SCALE
        image_ref[:, cols] = image
        low_ref[:, cols] = image.astype(bf16)


def own_kernel(blocks, own_ref, tiles_ref, part_ref):
    local_products(blocks, own_ref[:, : blocks * BLK], tiles_ref, part_ref)


def copy_kernel(columns, from_ref, to_ref):
    to_ref[...] = from_ref[:, :columns]


def second_kernel(
    blocks, a_ref, b_ref, tiles_ref, part_ref, noise_ref, vec_ref, image_ref,
    twice_ref, low_ref, sums_ref, wide_ref,
):
    width = vec_ref.shape[0]
    gather_sides(blocks, odd_place(), a_ref[...], b_ref[...], wide_ref)
    totals = [jnp.zeros((width, LANES), f32) for _ in range(SUMS)]
    for pair in range(blocks // 2):
        cols = pair_cols(pair)
        r = vec_ref[:, cols]
        w = image_ref[:, cols]
        q = noise_ref[:, cols] * w + (part_ref[:, cols] + side_products(blocks, pair, wide_ref, tiles_ref)) * SCALE
        twice_ref[:, cols] = q
        u = r - SHIFT * w
        y = w - SHIFT * q
        low_ref[:, cols] = y.astype(bf16)
        terms = (r * r, r * w, u * u, u * w, w * w, y * u, q * u, y * w, q * w)
        totals = [total + (term[:, :LANES] + term[:, LANES:]) for total, term in zip(totals, terms)]
    lane = lax.broadcasted_iota(jnp.int32, (width, LANES), 1)
    out = jnp.zeros((width, LANES), f32)
    for at, total in enumerate(totals):
        out = jnp.where(lane == at, jnp.sum(total, axis=1, keepdims=True), out)
    sums_ref[...] = out
    points = blocks * BLK
    for at, part in enumerate(three_parts(out)):
        low_ref[:, points + at * LANES : points + (at + 1) * LANES] = part.astype(bf16)


def third_kernel(blocks, a_ref, b_ref, tiles_ref, part_ref, out_ref, wide_ref):
    points = blocks * BLK
    gather_sides(blocks, odd_place(), a_ref[:, :points], b_ref[...], wide_ref)
    for pair in range(blocks // 2):
        cols = pair_cols(pair)
        out_ref[:, cols] = (part_ref[:, cols] + side_products(blocks, pair, wide_ref, tiles_ref)) * SCALE


def last_kernel(sums_ref, noise_ref, vec_ref, image_ref, twice_ref, prod_ref, x_ref, r_ref, w_ref):
    rr, rw, uu, uw, ww, yu, qu, yw, qw = [sums_ref[:, at : at + 1] for at in range(SUMS)]
    alpha0 = rr / rw
    delta = alpha0 - SHIFT
    norm = uu - 2.0 * delta * uw + delta * delta * ww
    curv = yu - delta * (qu + yw) + delta * delta * qw
    beta = norm / rr
    alpha1 = norm / (curv - beta * norm / alpha0)
    r0, w0, q0 = vec_ref[...], image_ref[...], twice_ref[...]
    r1 = r0 - alpha0 * w0
    w1 = w0 - alpha0 * q0
    share = alpha0 * (1.0 / SHIFT)
    q1 = noise_ref[...] * w1 + (1.0 - share) * (q0 - noise_ref[...] * w0) + share * prod_ref[...]
    x_ref[...] = alpha0 * r0 + alpha1 * (r1 + beta * r0)
    r_ref[...] = r1 - alpha1 * (w1 + beta * w0)
    w_ref[...] = w1 - alpha1 * (q1 + beta * q0)


def swap_pairs(count, first):
    pairs = []
    for low in range(first, count - 1, 2):
        pairs += [(low, low + 1), (low + 1, low)]
    return pairs


def first_side(x):
    return lax.ppermute(x, "pts", swap_pairs(lax.axis_size("pts"), 0))


def second_side(x):
    return lax.ppermute(x, "pts", swap_pairs(lax.axis_size("pts"), 1))


def both_sides(x):
    return first_side(x), second_side(x)


def total_over_points(x, neighbour):
    count = lax.axis_size("pts")
    if count & (count - 1):
        return lax.psum(x, "pts")
    if count == 1:
        return x
    high, middle, low = [
        neighbour[:, neighbour.shape[1] - (3 - k) * LANES :][:, :LANES].astype(f32) for k in range(3)
    ]
    x = x + ((high + middle) + low)
    step = count
    while step > 2:
        size = 4 if step > 4 else 2
        step //= size
        x = x + sum(
            lax.ppermute(x, "pts", [(i, i ^ (k * step)) for i in range(count)]) for k in range(1, size)
        )
    return x


VM = pl.BlockSpec(memory_space=pltpu.VMEM)
FAR = pl.BlockSpec(memory_space=pltpu.HBM)
SM = pl.BlockSpec(memory_space=pltpu.SMEM)


def per_device(points, noise_var, right_side, pattern):
    local_rows = points.shape[0]
    width = right_side.shape[0]
    blocks = local_rows // BLK
    assert blocks == REACH
    params = pltpu.CompilerParams(vmem_limit_bytes=12 * MIB)
    full = (width, local_rows)
    tiles_type = pltpu.VMEM((spare_slot(blocks) + 1, BLK, BLK), bf16)
    pairs = blocks * (blocks + 1) // 2

    def numbers(count):
        return pltpu.SMEM((count,), jnp.int32)

    lists = (
        pltpu.VMEM((blocks, BLK, LANES), bf16),
        numbers(pairs + STEPS[-1]),
    )
    wide = pltpu.VMEM((width, 2 * local_rows), bf16)

    def call(kernel, name, ins, outs, scratch=(), aliases=None, spaces=()):
        spaces = tuple(spaces) + (VM,) * (len(ins) - len(spaces))
        return pl.pallas_call(
            kernel,
            out_shape=outs,
            in_specs=list(spaces),
            out_specs=jax.tree.map(
                lambda x: SM if x.dtype == jnp.int32 else VM, outs, is_leaf=lambda x: hasattr(x, "dtype")
            ),
            scratch_shapes=list(scratch),
            input_output_aliases=aliases or {},
            compiler_params=params,
            cost_estimate=pl.CostEstimate(flops=10**9, bytes_accessed=10**7, transcendentals=0),
            name=name,
        )(*[pltpu.with_memory_space_constraint(x, space.memory_space) for x, space in zip(ins, spaces)])

    payload, vec, noise, listed = call(
        prep_kernel,
        "prep",
        (points.T, right_side, noise_var[None, :], pattern),
        (
            pltpu.VMEM((F + width, local_rows), bf16),
            pltpu.VMEM(full, f32),
            pltpu.VMEM((1, local_rows), f32),
            pltpu.SMEM(pattern.shape, jnp.int32),
        ),
        (pltpu.SemaphoreType.DMA((4,)),),
        spaces=(FAR,) * 4,
    )
    halo_a, halo_b = both_sides(payload)
    tiles, right, part = call(
        functools.partial(local_kernel, blocks),
        "local_tiles",
        (listed, payload),
        (tiles_type, pltpu.VMEM((blocks, LANES, BLK), bf16), pltpu.VMEM(full, f32)),
        lists,
        spaces=(SM,),
    )
    tiles = call(
        functools.partial(side_kernel, blocks),
        "side_tiles",
        (listed, halo_b, right, tiles),
        tiles_type,
        lists + (numbers(2),),
        {3: 0},
        spaces=(SM,),
    )
    tiles, image, low = call(
        functools.partial(first_kernel, blocks),
        "image",
        (listed, halo_a, halo_b, right, tiles, part, noise, vec),
        (tiles_type, pltpu.VMEM(full, f32), pltpu.VMEM(full, bf16)),
        lists + (numbers(2), wide),
        {4: 0},
        spaces=(SM,),
    )
    low_a, low_b = both_sides(low)
    part = call(
        functools.partial(own_kernel, blocks), "own_products", (low, tiles), pltpu.VMEM(full, f32)
    )
    twice, low, sums = call(
        functools.partial(second_kernel, blocks),
        "twice",
        (low_a, low_b, tiles, part, noise, vec, image),
        (
            pltpu.VMEM(full, f32),
            pltpu.VMEM((width, local_rows + 3 * LANES), bf16),
            pltpu.VMEM((width, LANES), f32),
        ),
        (wide,),
    )
    low_a = first_side(low)
    low_b = second_side(
        call(functools.partial(copy_kernel, local_rows), "second_message", (low,), pltpu.VMEM(full, bf16))
    )
    low, low_a = lax.optimization_barrier((low, low_a))
    sums = total_over_points(sums, low_a)
    part = call(functools.partial(own_kernel, blocks), "own_products_last", (low, tiles), pltpu.VMEM(full, f32))
    prods = call(
        functools.partial(third_kernel, blocks),
        "products",
        (low_a, low_b, tiles, part),
        pltpu.VMEM(full, f32),
        (wide,),
    )
    out = jax.ShapeDtypeStruct(full, f32)
    return call(last_kernel, "update", (sums, noise, vec, image, twice, prods), (out, out, out))


def solution(mesh):
    placed = (P("pts", None), P("pts"), P("rhs", "pts"), P("pts", None))
    return jax.shard_map(
        per_device,
        mesh=mesh,
        in_specs=placed,
        out_specs=(P("rhs", "pts"), P("rhs", "pts"), P("rhs", "pts")),
        check_vma=False,
    )
```

```python
import functools

import jax
import jax.numpy as jnp
from jax import lax
from jax.experimental import pallas as pl
from jax.experimental.pallas import tpu as pltpu
from jax.sharding import PartitionSpec as P

F = 32
BLK = 128
REACH = 16
WEXP = 18
LANES = 128
GAMMA = float(WEXP) ** (1.0 / (WEXP + 1))
GAMMA_SQ = GAMMA * GAMMA
OFFSET = GAMMA * (WEXP + 1) / WEXP
TINY = 1e-30
SCALE = 1.0 / (4 * BLK)
SHIFT = 2.0 / (0.5 + 0.6)
SUMS = 9
STEPS = (48, 16, 8)
FIELD = 10
MIB = 1 << 20

f32 = jnp.float32
bf16 = jnp.bfloat16


def rounded(x):
    return x.astype(bf16).astype(f32)


def three_parts(x):
    high = rounded(x)
    rest = x - high
    middle = rounded(rest)
    return high, middle, rounded(rest - middle)


def eight_rows(rows):
    row = lax.broadcasted_iota(jnp.int32, (8, rows[0].shape[1]), 0)
    out = jnp.zeros((8, rows[0].shape[1]), f32)
    for at, value in enumerate(rows):
        out = jnp.where(row == at, value, out)
    return out


def fill_features(points, left_ref, first, right_ref=None):
    x = points.astype(f32)
    count = x.shape[1]
    squares = three_parts(GAMMA_SQ * jnp.sum(x * x, axis=0, keepdims=True))
    ones = [jnp.ones((1, count), f32)] * 3
    blank = jnp.zeros((LANES - 3 * F - 8, count), f32)
    left = jnp.concatenate([x, x, x, eight_rows(list(squares) + ones), blank], axis=0).astype(bf16)
    for b in range(count // BLK):
        left_ref[first + b] = left[:, b * BLK : (b + 1) * BLK].T
    if right_ref is not None:
        cross = three_parts((-2.0 * GAMMA_SQ) * x)
        right = jnp.concatenate(list(cross) + [eight_rows(ones + list(squares)), blank], axis=0).astype(bf16)
        for b in range(count // BLK):
            right_ref[b] = right[:, b * BLK : (b + 1) * BLK]


def tile_values(left, right):
    scaled = jnp.dot(left, right, preferred_element_type=f32)
    scaled = jnp.maximum(scaled, TINY)
    s = jnp.maximum(GAMMA - scaled * lax.rsqrt(scaled), 0.0)
    s2 = s * s
    s4 = s2 * s2
    s8 = s4 * s4
    s16 = s8 * s8
    return ((s16 * s2) * (OFFSET - s)).astype(bf16)


def entry(slot, mirror, other, home):
    return (((((home << 5) + other) << FIELD) + mirror) << FIELD) + slot


def make_tiles(first, count, list_ref, left_ref, right_ref, tiles_ref, mirrored):
    mask = (1 << FIELD) - 1

    def one(at):
        code = list_ref[first + at]
        home = code >> (2 * FIELD + 5)
        other = (code >> (2 * FIELD)) & 31
        tile = tile_values(left_ref[other], right_ref[home])
        if mirrored:
            tiles_ref[(code >> FIELD) & mask] = tile.T
        tiles_ref[code & mask] = tile

    done = jnp.int32(0)
    for size in STEPS:

        def step(at, carry, size=size, done=done):
            for k in range(size):
                one(done + at * size + k)
            return carry

        last = size == STEPS[-1]
        steps = (count - done + (size - 1 if last else 0)) // size
        lax.fori_loop(0, steps, step, 0)
        done = done + steps * size


def local_slot(blocks, home, other):
    return ((home // 2) * blocks + other) * 2 + home % 2


def side_slot(blocks, home, other, after):
    wide = other - 2 * (home // 2) + (blocks if after else 0)
    return blocks * blocks + ((home // 2) * (blocks + 2) + wide) * 2 + home % 2


def spare_slot(blocks):
    return 2 * blocks * (blocks + 1)


def local_entries(blocks):
    return [(a, b, REACH + b - a) for a in range(blocks) for b in range(a, blocks)]


def side_entries(blocks, after):
    if after:
        return [(a, b, 2 * REACH + b - a) for a in range(blocks) for b in range(a + 1)]
    return [(a, b, b - a) for a in range(blocks) for b in range(a, blocks)]


def pad_list(end, list_ref, spare):
    for k in range(STEPS[-1] - 1):
        list_ref[end + k] = jnp.int32(entry(spare, spare, 0, 0))


def clear_tiles(first, last, list_ref, tiles_ref, mirrored):
    mask = (1 << FIELD) - 1

    def step(at, carry):
        code = list_ref[at]
        tiles_ref[code & mask] = jnp.zeros((BLK, BLK), bf16)
        if mirrored:
            tiles_ref[(code >> FIELD) & mask] = jnp.zeros((BLK, BLK), bf16)
        return carry

    lax.fori_loop(first, last, step, 0)


def products(vec, tiles_ref, first, wide):
    tiles = tiles_ref[first : first + 2 * wide].reshape(wide, 2, BLK, BLK)
    tiles = jnp.concatenate([tiles[:, 0].reshape(wide * BLK, BLK), tiles[:, 1].reshape(wide * BLK, BLK)], axis=1)
    return jnp.dot(vec, tiles, preferred_element_type=f32)


def pair_cols(pair):
    return slice(pair * 2 * BLK, (pair + 1) * 2 * BLK)


def local_products(blocks, vec, tiles_ref, out_ref):
    for pair in range(blocks // 2):
        out_ref[:, pair_cols(pair)] = products(vec, tiles_ref, pair * 2 * blocks, blocks)


def gather_sides(blocks, before, side_a, side_b, wide_ref):
    size = blocks * BLK
    at_a = pl.multiple_of(jnp.where(before == 1, 0, size), size)
    at_b = pl.multiple_of(size - at_a, size)
    wide_ref[:, pl.ds(at_a, size)] = side_a
    wide_ref[:, pl.ds(at_b, size)] = side_b


def side_products(blocks, pair, wide_ref, tiles_ref):
    vec = wide_ref[:, pair * 2 * BLK : (pair * 2 + blocks + 2) * BLK]
    return products(vec, tiles_ref, blocks * blocks + pair * 2 * (blocks + 2), blocks + 2)


def odd_place():
    return lax.rem(lax.axis_index("pts"), 2)


def prep_kernel(points_ref, vec_ref, noise_ref, pattern_ref, out_ref, near_vec_ref, near_noise_ref, listed_ref, sems):
    points_copy = pltpu.make_async_copy(points_ref, out_ref.at[:F], sems.at[0])
    vec_copy = pltpu.make_async_copy(vec_ref, near_vec_ref, sems.at[1])
    noise_copy = pltpu.make_async_copy(noise_ref, near_noise_ref, sems.at[2])
    vec_copy.start()
    points_copy.start()
    noise_copy.start()
    pattern_copy = pltpu.make_async_copy(pattern_ref, listed_ref, sems.at[3])
    pattern_copy.start()
    vec_copy.wait()
    out_ref[F:, :] = near_vec_ref[...].astype(bf16)
    points_copy.wait()
    noise_copy.wait()
    pattern_copy.wait()


def local_kernel(
    blocks, listed_ref, own_ref, tiles_ref, right_ref, part_ref, side_list_ref, left_ref, list_ref
):
    fill_features(own_ref[:F, :], left_ref, 0, right_ref)
    for pair in range(blocks // 2):
        first = blocks * blocks + pair * 2 * (blocks + 2)
        tiles_ref[first + 1] = jnp.zeros((BLK, BLK), bf16)
        tiles_ref[first + 2 * (blocks + 1)] = jnp.zeros((BLK, BLK), bf16)
    entries = [
        (entry(local_slot(blocks, home, other), local_slot(blocks, other, home), other, home), home, column)
        for home, other, column in local_entries(blocks)
    ]
    count = scan_entries(entries, listed_ref, list_ref, 0)
    clear_tiles(count + STEPS[-1], list_ref.shape[0], list_ref, tiles_ref, True)
    pad_list(count, list_ref, spare_slot(blocks))
    make_tiles(0, count, list_ref, left_ref, right_ref, tiles_ref, True)
    for row, after in enumerate((True, False)):
        entries = []
        for home, other, column in side_entries(blocks, after):
            slot = side_slot(blocks, home, other, after)
            entries.append((entry(slot, slot, other, home), home, column))
        size = len(entries) + STEPS[-1]
        side_count = scan_entries(entries, listed_ref, side_list_ref, row * size)
        side_list_ref[2 * size + row] = side_count
        pad_list(row * size + side_count, side_list_ref, spare_slot(blocks))
    local_products(blocks, own_ref[F:, :], tiles_ref, part_ref)


def scan_entries(entries, listed_ref, list_ref, first):
    size = len(entries) + STEPS[-1]
    count = jnp.int32(0)
    for at, (code, home, column) in enumerate(entries):
        live = listed_ref[home, column]
        list_ref[first + jnp.where(live == 1, count, size - 1 - at + count)] = jnp.int32(code)
        count = count + live
    return count


def make_side(blocks, before, side_list_ref, points, right_ref, tiles_ref, left_ref):
    size = blocks * (blocks + 1) // 2 + STEPS[-1]
    first = before * size
    count = side_list_ref[2 * size + before]
    clear_tiles(first + count + STEPS[-1], first + size, side_list_ref, tiles_ref, False)
    fill_features(points, left_ref, 0)
    make_tiles(first, count, side_list_ref, left_ref, right_ref, tiles_ref, False)


def side_kernel(blocks, side_list_ref, b_ref, right_ref, tiles_in, tiles_ref, left_ref):
    del tiles_in
    make_side(blocks, 1 - odd_place(), side_list_ref, b_ref[:F, :], right_ref, tiles_ref, left_ref)


def first_kernel(
    blocks, side_list_ref, a_ref, b_ref, right_ref, tiles_in, part_ref, noise_ref, vec_ref,
    tiles_ref, image_ref, low_ref, left_ref, wide_ref,
):
    del tiles_in
    before = odd_place()
    make_side(blocks, before, side_list_ref, a_ref[:F, :], right_ref, tiles_ref, left_ref)
    gather_sides(blocks, before, a_ref[F:, :], b_ref[F:, :], wide_ref)
    for pair in range(blocks // 2):
        cols = pair_cols(pair)
        total = part_ref[:, cols] + side_products(blocks, pair, wide_ref, tiles_ref)
        image = noise_ref[:, cols] * vec_ref[:, cols] + total * SCALE
        image_ref[:, cols] = image
        low_ref[:, cols] = image.astype(bf16)


def own_kernel(blocks, own_ref, tiles_ref, part_ref):
    local_products(blocks, own_ref[:, : blocks * BLK], tiles_ref, part_ref)


def copy_kernel(columns, from_ref, to_ref):
    to_ref[...] = from_ref[:, :columns]


def second_kernel(
    blocks, a_ref, b_ref, tiles_ref, part_ref, noise_ref, vec_ref, image_ref,
    twice_ref, low_ref, sums_ref, wide_ref,
):
    width = vec_ref.shape[0]
    gather_sides(blocks, odd_place(), a_ref[...], b_ref[...], wide_ref)
    totals = [jnp.zeros((width, LANES), f32) for _ in range(SUMS)]
    for pair in range(blocks // 2):
        cols = pair_cols(pair)
        r = vec_ref[:, cols]
        w = image_ref[:, cols]
        q = noise_ref[:, cols] * w + (part_ref[:, cols] + side_products(blocks, pair, wide_ref, tiles_ref)) * SCALE
        twice_ref[:, cols] = q
        u = r - SHIFT * w
        y = w - SHIFT * q
        low_ref[:, cols] = y.astype(bf16)
        terms = (r * r, r * w, u * u, u * w, w * w, y * u, q * u, y * w, q * w)
        totals = [total + (term[:, :LANES] + term[:, LANES:]) for total, term in zip(totals, terms)]
    lane = lax.broadcasted_iota(jnp.int32, (width, LANES), 1)
    out = jnp.zeros((width, LANES), f32)
    for at, total in enumerate(totals):
        out = jnp.where(lane == at, jnp.sum(total, axis=1, keepdims=True), out)
    sums_ref[...] = out
    points = blocks * BLK
    for at, part in enumerate(three_parts(out)):
        low_ref[:, points + at * LANES : points + (at + 1) * LANES] = part.astype(bf16)


def third_kernel(blocks, a_ref, b_ref, tiles_ref, part_ref, out_ref, wide_ref):
    points = blocks * BLK
    gather_sides(blocks, odd_place(), a_ref[:, :points], b_ref[...], wide_ref)
    for pair in range(blocks // 2):
        cols = pair_cols(pair)
        out_ref[:, cols] = (part_ref[:, cols] + side_products(blocks, pair, wide_ref, tiles_ref)) * SCALE


def last_kernel(sums_ref, noise_ref, vec_ref, image_ref, twice_ref, prod_ref, x_ref, r_ref, w_ref):
    rr, rw, uu, uw, ww, yu, qu, yw, qw = [sums_ref[:, at : at + 1] for at in range(SUMS)]
    alpha0 = rr / rw
    delta = alpha0 - SHIFT
    norm = uu - 2.0 * delta * uw + delta * delta * ww
    curv = yu - delta * (qu + yw) + delta * delta * qw
    beta = norm / rr
    alpha1 = norm / (curv - beta * norm / alpha0)
    r0, w0, q0 = vec_ref[...], image_ref[...], twice_ref[...]
    r1 = r0 - alpha0 * w0
    w1 = w0 - alpha0 * q0
    share = alpha0 * (1.0 / SHIFT)
    q1 = noise_ref[...] * w1 + (1.0 - share) * (q0 - noise_ref[...] * w0) + share * prod_ref[...]
    x_ref[...] = alpha0 * r0 + alpha1 * (r1 + beta * r0)
    r_ref[...] = r1 - alpha1 * (w1 + beta * w0)
    w_ref[...] = w1 - alpha1 * (q1 + beta * q0)


def swap_pairs(count, first):
    pairs = []
    for low in range(first, count - 1, 2):
        pairs += [(low, low + 1), (low + 1, low)]
    return pairs


def first_side(x):
    return lax.ppermute(x, "pts", swap_pairs(lax.axis_size("pts"), 0))


def second_side(x):
    return lax.ppermute(x, "pts", swap_pairs(lax.axis_size("pts"), 1))


def both_sides(x):
    return first_side(x), second_side(x)


def total_over_points(x, neighbour):
    count = lax.axis_size("pts")
    if count & (count - 1):
        return lax.psum(x, "pts")
    if count == 1:
        return x
    high, middle, low = [
        neighbour[:, neighbour.shape[1] - (3 - k) * LANES :][:, :LANES].astype(f32) for k in range(3)
    ]
    x = x + ((high + middle) + low)
    step = 2
    while step < count:
        x = x + lax.ppermute(x, "pts", [(i, i ^ step) for i in range(count)])
        step *= 2
    return x


VM = pl.BlockSpec(memory_space=pltpu.VMEM)
FAR = pl.BlockSpec(memory_space=pltpu.HBM)
SM = pl.BlockSpec(memory_space=pltpu.SMEM)


def per_device(points, noise_var, right_side, pattern):
    local_rows = points.shape[0]
    width = right_side.shape[0]
    blocks = local_rows // BLK
    assert blocks == REACH
    params = pltpu.CompilerParams(vmem_limit_bytes=12 * MIB)
    full = (width, local_rows)
    tiles_type = pltpu.VMEM((spare_slot(blocks) + 1, BLK, BLK), bf16)
    pairs = blocks * (blocks + 1) // 2

    def numbers(count):
        return pltpu.SMEM((count,), jnp.int32)

    left = pltpu.VMEM((blocks, BLK, LANES), bf16)
    wide = pltpu.VMEM((width, 2 * local_rows), bf16)

    def call(kernel, name, ins, outs, scratch=(), aliases=None, spaces=()):
        spaces = tuple(spaces) + (VM,) * (len(ins) - len(spaces))
        return pl.pallas_call(
            kernel,
            out_shape=outs,
            in_specs=list(spaces),
            out_specs=jax.tree.map(
                lambda x: SM if x.dtype == jnp.int32 else VM, outs, is_leaf=lambda x: hasattr(x, "dtype")
            ),
            scratch_shapes=list(scratch),
            input_output_aliases=aliases or {},
            compiler_params=params,
            cost_estimate=pl.CostEstimate(flops=10**9, bytes_accessed=10**7, transcendentals=0),
            name=name,
        )(*[pltpu.with_memory_space_constraint(x, space.memory_space) for x, space in zip(ins, spaces)])

    payload, vec, noise, listed = call(
        prep_kernel,
        "prep",
        (points.T, right_side, noise_var[None, :], pattern),
        (
            pltpu.VMEM((F + width, local_rows), bf16),
            pltpu.VMEM(full, f32),
            pltpu.VMEM((1, local_rows), f32),
            pltpu.SMEM(pattern.shape, jnp.int32),
        ),
        (pltpu.SemaphoreType.DMA((4,)),),
        spaces=(FAR,) * 4,
    )
    halo_a, halo_b = both_sides(payload)
    tiles, right, part, side_list = call(
        functools.partial(local_kernel, blocks),
        "local_tiles",
        (listed, payload),
        (
            tiles_type,
            pltpu.VMEM((blocks, LANES, BLK), bf16),
            pltpu.VMEM(full, f32),
            numbers(2 * (pairs + STEPS[-1]) + 2),
        ),
        (left, numbers(pairs + STEPS[-1])),
        spaces=(SM,),
    )
    tiles = call(
        functools.partial(side_kernel, blocks),
        "side_tiles",
        (side_list, halo_b, right, tiles),
        tiles_type,
        (left,),
        {3: 0},
        spaces=(SM,),
    )
    tiles, image, low = call(
        functools.partial(first_kernel, blocks),
        "image",
        (side_list, halo_a, halo_b, right, tiles, part, noise, vec),
        (tiles_type, pltpu.VMEM(full, f32), pltpu.VMEM(full, bf16)),
        (left, wide),
        {4: 0},
        spaces=(SM,),
    )
    low_a, low_b = both_sides(low)
    part = call(
        functools.partial(own_kernel, blocks), "own_products", (low, tiles), pltpu.VMEM(full, f32)
    )
    twice, low, sums = call(
        functools.partial(second_kernel, blocks),
        "twice",
        (low_a, low_b, tiles, part, noise, vec, image),
        (
            pltpu.VMEM(full, f32),
            pltpu.VMEM((width, local_rows + 3 * LANES), bf16),
            pltpu.VMEM((width, LANES), f32),
        ),
        (wide,),
    )
    low_a = first_side(low)
    low_b = second_side(
        call(functools.partial(copy_kernel, local_rows), "second_message", (low,), pltpu.VMEM(full, bf16))
    )
    low, low_a = lax.optimization_barrier((low, low_a))
    sums = total_over_points(sums, low_a)
    part = call(functools.partial(own_kernel, blocks), "own_products_last", (low, tiles), pltpu.VMEM(full, f32))
    prods = call(
        functools.partial(third_kernel, blocks),
        "products",
        (low_a, low_b, tiles, part),
        pltpu.VMEM(full, f32),
        (wide,),
    )
    out = jax.ShapeDtypeStruct(full, f32)
    return call(last_kernel, "update", (sums, noise, vec, image, twice, prods), (out, out, out))


def solution(mesh):
    placed = (P("pts", None), P("pts"), P("rhs", "pts"), P("pts", None))
    return jax.shard_map(
        per_device,
        mesh=mesh,
        in_specs=placed,
        out_specs=(P("rhs", "pts"), P("rhs", "pts"), P("rhs", "pts")),
        check_vma=False,
    )
```

```python
import functools

import jax
import jax.numpy as jnp
from jax import lax
from jax.experimental import pallas as pl
from jax.experimental.pallas import tpu as pltpu
from jax.sharding import PartitionSpec as P

F = 32
BLK = 128
REACH = 16
WEXP = 18
LANES = 128
GAMMA = float(WEXP) ** (1.0 / (WEXP + 1))
GAMMA_SQ = GAMMA * GAMMA
OFFSET = GAMMA * (WEXP + 1) / WEXP
TINY = 1e-30
SCALE = 1.0 / (4 * BLK)
SHIFT = 2.0 / (0.5 + 0.6)
SUMS = 9
STEPS = (48, 16, 8)
FIELD = 10
MIB = 1 << 20

f32 = jnp.float32
bf16 = jnp.bfloat16


def rounded(x):
    return x.astype(bf16).astype(f32)


def three_parts(x):
    high = rounded(x)
    rest = x - high
    middle = rounded(rest)
    return high, middle, rounded(rest - middle)


def eight_rows(rows):
    row = lax.broadcasted_iota(jnp.int32, (8, rows[0].shape[1]), 0)
    out = jnp.zeros((8, rows[0].shape[1]), f32)
    for at, value in enumerate(rows):
        out = jnp.where(row == at, value, out)
    return out


def fill_features(points, left_ref, first, right_ref=None):
    x = points.astype(f32)
    count = x.shape[1]
    squares = three_parts(GAMMA_SQ * jnp.sum(x * x, axis=0, keepdims=True))
    ones = [jnp.ones((1, count), f32)] * 3
    blank = jnp.zeros((LANES - 3 * F - 8, count), f32)
    left = jnp.concatenate([x, x, x, eight_rows(list(squares) + ones), blank], axis=0).astype(bf16)
    for b in range(count // BLK):
        left_ref[first + b] = left[:, b * BLK : (b + 1) * BLK].T
    if right_ref is not None:
        cross = three_parts((-2.0 * GAMMA_SQ) * x)
        right = jnp.concatenate(list(cross) + [eight_rows(ones + list(squares)), blank], axis=0).astype(bf16)
        for b in range(count // BLK):
            right_ref[b] = right[:, b * BLK : (b + 1) * BLK]


def tile_values(left, right):
    scaled = jnp.dot(left, right, preferred_element_type=f32)
    scaled = jnp.maximum(scaled, TINY)
    s = jnp.maximum(GAMMA - scaled * lax.rsqrt(scaled), 0.0)
    s2 = s * s
    s4 = s2 * s2
    s8 = s4 * s4
    s16 = s8 * s8
    return ((s16 * s2) * (OFFSET - s)).astype(bf16)


def entry(slot, mirror, other, home):
    return (((((home << 5) + other) << FIELD) + mirror) << FIELD) + slot


def make_tiles(first, count, list_ref, left_ref, right_ref, tiles_ref, mirrored):
    mask = (1 << FIELD) - 1

    def one(at):
        code = list_ref[first + at]
        home = code >> (2 * FIELD + 5)
        other = (code >> (2 * FIELD)) & 31
        tile = tile_values(left_ref[other], right_ref[home])
        if mirrored:
            tiles_ref[(code >> FIELD) & mask] = tile.T
        tiles_ref[code & mask] = tile

    done = jnp.int32(0)
    for size in STEPS:

        def step(at, carry, size=size, done=done):
            for k in range(size):
                one(done + at * size + k)
            return carry

        last = size == STEPS[-1]
        steps = (count - done + (size - 1 if last else 0)) // size
        lax.fori_loop(0, steps, step, 0)
        done = done + steps * size


def local_slot(blocks, home, other):
    return ((home // 2) * blocks + other) * 2 + home % 2


def side_slot(blocks, home, other, after):
    wide = other - 2 * (home // 2) + (blocks if after else 0)
    return blocks * blocks + ((home // 2) * (blocks + 2) + wide) * 2 + home % 2


def spare_slot(blocks):
    return 2 * blocks * (blocks + 1)


def local_entries(blocks):
    return [(a, b, REACH + b - a) for a in range(blocks) for b in range(a, blocks)]


def side_entries(blocks, after):
    if after:
        return [(a, b, 2 * REACH + b - a) for a in range(blocks) for b in range(a + 1)]
    return [(a, b, b - a) for a in range(blocks) for b in range(a, blocks)]


def pad_list(end, list_ref, spare):
    for k in range(STEPS[-1] - 1):
        list_ref[end + k] = jnp.int32(entry(spare, spare, 0, 0))


def clear_tiles(first, last, list_ref, tiles_ref, mirrored):
    mask = (1 << FIELD) - 1

    def step(at, carry):
        code = list_ref[at]
        tiles_ref[code & mask] = jnp.zeros((BLK, BLK), bf16)
        if mirrored:
            tiles_ref[(code >> FIELD) & mask] = jnp.zeros((BLK, BLK), bf16)
        return carry

    lax.fori_loop(first, last, step, 0)


def products(vec, tiles_ref, first, wide):
    tiles = tiles_ref[first : first + 2 * wide].reshape(wide, 2, BLK, BLK)
    tiles = jnp.concatenate([tiles[:, 0].reshape(wide * BLK, BLK), tiles[:, 1].reshape(wide * BLK, BLK)], axis=1)
    return jnp.dot(vec, tiles, preferred_element_type=f32)


def pair_cols(pair):
    return slice(pair * 2 * BLK, (pair + 1) * 2 * BLK)


def local_products(blocks, vec, tiles_ref, out_ref):
    for pair in range(blocks // 2):
        out_ref[:, pair_cols(pair)] = products(vec, tiles_ref, pair * 2 * blocks, blocks)


def gather_sides(blocks, before, side_a, side_b, wide_ref):
    size = blocks * BLK
    at_a = pl.multiple_of(jnp.where(before == 1, 0, size), size)
    at_b = pl.multiple_of(size - at_a, size)
    wide_ref[:, pl.ds(at_a, size)] = side_a
    wide_ref[:, pl.ds(at_b, size)] = side_b


def side_products(blocks, pair, wide_ref, tiles_ref):
    vec = wide_ref[:, pair * 2 * BLK : (pair * 2 + blocks + 2) * BLK]
    return products(vec, tiles_ref, blocks * blocks + pair * 2 * (blocks + 2), blocks + 2)


def odd_place():
    return lax.rem(lax.axis_index("pts"), 2)


def prep_kernel(points_ref, vec_ref, noise_ref, pattern_ref, out_ref, near_vec_ref, near_noise_ref, listed_ref, sems):
    points_copy = pltpu.make_async_copy(points_ref, out_ref.at[:F], sems.at[0])
    vec_copy = pltpu.make_async_copy(vec_ref, near_vec_ref, sems.at[1])
    noise_copy = pltpu.make_async_copy(noise_ref, near_noise_ref, sems.at[2])
    vec_copy.start()
    points_copy.start()
    noise_copy.start()
    pattern_copy = pltpu.make_async_copy(pattern_ref, listed_ref, sems.at[3])
    pattern_copy.start()
    vec_copy.wait()
    out_ref[F:, :] = near_vec_ref[...].astype(bf16)
    points_copy.wait()
    noise_copy.wait()
    pattern_copy.wait()


def local_kernel(
    blocks, listed_ref, own_ref, tiles_ref, right_ref, part_ref, side_list_ref, left_ref, list_ref
):
    fill_features(own_ref[:F, :], left_ref, 0, right_ref)
    for pair in range(blocks // 2):
        first = blocks * blocks + pair * 2 * (blocks + 2)
        tiles_ref[first + 1] = jnp.zeros((BLK, BLK), bf16)
        tiles_ref[first + 2 * (blocks + 1)] = jnp.zeros((BLK, BLK), bf16)
    entries = [
        (entry(local_slot(blocks, home, other), local_slot(blocks, other, home), other, home), home, column)
        for home, other, column in local_entries(blocks)
    ]
    count = scan_entries(entries, listed_ref, list_ref, 0)
    clear_tiles(count + STEPS[-1], list_ref.shape[0], list_ref, tiles_ref, True)
    pad_list(count, list_ref, spare_slot(blocks))
    make_tiles(0, count, list_ref, left_ref, right_ref, tiles_ref, True)
    for row, after in enumerate((True, False)):
        entries = []
        for home, other, column in side_entries(blocks, after):
            slot = side_slot(blocks, home, other, after)
            entries.append((entry(slot, slot, other, home), home, column))
        size = len(entries) + STEPS[-1]
        side_count = scan_entries(entries, listed_ref, side_list_ref, row * size)
        side_list_ref[2 * size + row] = side_count
        pad_list(row * size + side_count, side_list_ref, spare_slot(blocks))
    local_products(blocks, own_ref[F:, :], tiles_ref, part_ref)


def scan_entries(entries, listed_ref, list_ref, first):
    size = len(entries) + STEPS[-1]
    count = jnp.int32(0)
    for at, (code, home, column) in enumerate(entries):
        live = listed_ref[home, column]
        list_ref[first + jnp.where(live == 1, count, size - 1 - at + count)] = jnp.int32(code)
        count = count + live
    return count


def make_side(blocks, before, side_list_ref, points, right_ref, tiles_ref, left_ref):
    size = blocks * (blocks + 1) // 2 + STEPS[-1]
    first = before * size
    count = side_list_ref[2 * size + before]
    clear_tiles(first + count + STEPS[-1], first + size, side_list_ref, tiles_ref, False)
    fill_features(points, left_ref, 0)
    make_tiles(first, count, side_list_ref, left_ref, right_ref, tiles_ref, False)


def side_kernel(blocks, side_list_ref, b_ref, right_ref, tiles_in, tiles_ref, left_ref):
    del tiles_in
    make_side(blocks, 1 - odd_place(), side_list_ref, b_ref[:F, :], right_ref, tiles_ref, left_ref)


def first_kernel(
    blocks, side_list_ref, a_ref, b_ref, right_ref, tiles_in, part_ref, noise_ref, vec_ref,
    tiles_ref, image_ref, low_ref, left_ref, wide_ref,
):
    del tiles_in
    before = odd_place()
    make_side(blocks, before, side_list_ref, a_ref[:F, :], right_ref, tiles_ref, left_ref)
    gather_sides(blocks, before, a_ref[F:, :], b_ref[F:, :], wide_ref)
    for pair in range(blocks // 2):
        cols = pair_cols(pair)
        total = part_ref[:, cols] + side_products(blocks, pair, wide_ref, tiles_ref)
        image = noise_ref[:, cols] * vec_ref[:, cols] + total * SCALE
        image_ref[:, cols] = image
        low_ref[:, cols] = image.astype(bf16)


def own_kernel(blocks, own_ref, tiles_ref, part_ref):
    local_products(blocks, own_ref[:, : blocks * BLK], tiles_ref, part_ref)


def copy_kernel(columns, from_ref, to_ref):
    to_ref[...] = from_ref[:, :columns]


def second_kernel(
    blocks, a_ref, b_ref, tiles_ref, part_ref, noise_ref, vec_ref, image_ref,
    twice_ref, low_ref, sums_ref, wide_ref,
):
    width = vec_ref.shape[0]
    gather_sides(blocks, odd_place(), a_ref[...], b_ref[...], wide_ref)
    totals = [jnp.zeros((width, LANES), f32) for _ in range(SUMS)]
    for pair in range(blocks // 2):
        cols = pair_cols(pair)
        r = vec_ref[:, cols]
        w = image_ref[:, cols]
        q = noise_ref[:, cols] * w + (part_ref[:, cols] + side_products(blocks, pair, wide_ref, tiles_ref)) * SCALE
        twice_ref[:, cols] = q
        u = r - SHIFT * w
        y = w - SHIFT * q
        low_ref[:, cols] = y.astype(bf16)
        terms = (r * r, r * w, u * u, u * w, w * w, y * u, q * u, y * w, q * w)
        totals = [total + (term[:, :LANES] + term[:, LANES:]) for total, term in zip(totals, terms)]
    lane = lax.broadcasted_iota(jnp.int32, (width, LANES), 1)
    out = jnp.zeros((width, LANES), f32)
    for at, total in enumerate(totals):
        out = jnp.where(lane == at, jnp.sum(total, axis=1, keepdims=True), out)
    sums_ref[...] = out
    points = blocks * BLK
    for at, part in enumerate(three_parts(out)):
        low_ref[:, points + at * LANES : points + (at + 1) * LANES] = part.astype(bf16)


def third_kernel(blocks, a_ref, b_ref, tiles_ref, part_ref, out_ref, wide_ref):
    points = blocks * BLK
    gather_sides(blocks, odd_place(), a_ref[:, :points], b_ref[...], wide_ref)
    for pair in range(blocks // 2):
        cols = pair_cols(pair)
        out_ref[:, cols] = (part_ref[:, cols] + side_products(blocks, pair, wide_ref, tiles_ref)) * SCALE


def last_kernel(sums_ref, noise_ref, vec_ref, image_ref, twice_ref, prod_ref, x_ref, r_ref, w_ref):
    width, points = vec_ref.shape
    rr, rw, uu, uw, ww, yu, qu, yw, qw = [
        jnp.broadcast_to(sums_ref[:, at : at + 1], (width, LANES)) for at in range(SUMS)
    ]
    alpha0 = rr / rw
    delta = alpha0 - SHIFT
    norm = uu - 2.0 * delta * uw + delta * delta * ww
    curv = yu - delta * (qu + yw) + delta * delta * qw
    beta = norm / rr
    alpha1 = norm / (curv - beta * norm / alpha0)
    share = alpha0 * (1.0 / SHIFT)
    for at in range(0, points, LANES):
        cols = slice(at, at + LANES)
        r0, w0, q0, noise = vec_ref[:, cols], image_ref[:, cols], twice_ref[:, cols], noise_ref[:, cols]
        r1 = r0 - alpha0 * w0
        w1 = w0 - alpha0 * q0
        q1 = noise * w1 + (1.0 - share) * (q0 - noise * w0) + share * prod_ref[:, cols]
        x_ref[:, cols] = alpha0 * r0 + alpha1 * (r1 + beta * r0)
        r_ref[:, cols] = r1 - alpha1 * (w1 + beta * w0)
        w_ref[:, cols] = w1 - alpha1 * (q1 + beta * q0)


def swap_pairs(count, first):
    pairs = []
    for low in range(first, count - 1, 2):
        pairs += [(low, low + 1), (low + 1, low)]
    return pairs


def first_side(x):
    return lax.ppermute(x, "pts", swap_pairs(lax.axis_size("pts"), 0))


def second_side(x):
    return lax.ppermute(x, "pts", swap_pairs(lax.axis_size("pts"), 1))


def both_sides(x):
    return first_side(x), second_side(x)


def total_over_points(x, neighbour):
    count = lax.axis_size("pts")
    if count & (count - 1):
        return lax.psum(x, "pts")
    if count == 1:
        return x
    high, middle, low = [
        neighbour[:, neighbour.shape[1] - (3 - k) * LANES :][:, :LANES].astype(f32) for k in range(3)
    ]
    x = x + ((high + middle) + low)
    step = 2
    while step < count:
        x = x + lax.ppermute(x, "pts", [(i, i ^ step) for i in range(count)])
        step *= 2
    return x


VM = pl.BlockSpec(memory_space=pltpu.VMEM)
FAR = pl.BlockSpec(memory_space=pltpu.HBM)
SM = pl.BlockSpec(memory_space=pltpu.SMEM)


def per_device(points, noise_var, right_side, pattern):
    local_rows = points.shape[0]
    width = right_side.shape[0]
    blocks = local_rows // BLK
    assert blocks == REACH
    params = pltpu.CompilerParams(vmem_limit_bytes=12 * MIB)
    full = (width, local_rows)
    tiles_type = pltpu.VMEM((spare_slot(blocks) + 1, BLK, BLK), bf16)
    pairs = blocks * (blocks + 1) // 2

    def numbers(count):
        return pltpu.SMEM((count,), jnp.int32)

    left = pltpu.VMEM((blocks, BLK, LANES), bf16)
    wide = pltpu.VMEM((width, 2 * local_rows), bf16)

    def call(kernel, name, ins, outs, scratch=(), aliases=None, spaces=()):
        spaces = tuple(spaces) + (VM,) * (len(ins) - len(spaces))
        return pl.pallas_call(
            kernel,
            out_shape=outs,
            in_specs=list(spaces),
            out_specs=jax.tree.map(
                lambda x: SM if x.dtype == jnp.int32 else VM, outs, is_leaf=lambda x: hasattr(x, "dtype")
            ),
            scratch_shapes=list(scratch),
            input_output_aliases=aliases or {},
            compiler_params=params,
            cost_estimate=pl.CostEstimate(flops=10**9, bytes_accessed=10**7, transcendentals=0),
            name=name,
        )(*[pltpu.with_memory_space_constraint(x, space.memory_space) for x, space in zip(ins, spaces)])

    payload, vec, noise, listed = call(
        prep_kernel,
        "prep",
        (points.T, right_side, noise_var[None, :], pattern),
        (
            pltpu.VMEM((F + width, local_rows), bf16),
            pltpu.VMEM(full, f32),
            pltpu.VMEM((1, local_rows), f32),
            pltpu.SMEM(pattern.shape, jnp.int32),
        ),
        (pltpu.SemaphoreType.DMA((4,)),),
        spaces=(FAR,) * 4,
    )
    halo_a, halo_b = both_sides(payload)
    tiles, right, part, side_list = call(
        functools.partial(local_kernel, blocks),
        "local_tiles",
        (listed, payload),
        (
            tiles_type,
            pltpu.VMEM((blocks, LANES, BLK), bf16),
            pltpu.VMEM(full, f32),
            numbers(2 * (pairs + STEPS[-1]) + 2),
        ),
        (left, numbers(pairs + STEPS[-1])),
        spaces=(SM,),
    )
    tiles = call(
        functools.partial(side_kernel, blocks),
        "side_tiles",
        (side_list, halo_b, right, tiles),
        tiles_type,
        (left,),
        {3: 0},
        spaces=(SM,),
    )
    tiles, image, low = call(
        functools.partial(first_kernel, blocks),
        "image",
        (side_list, halo_a, halo_b, right, tiles, part, noise, vec),
        (tiles_type, pltpu.VMEM(full, f32), pltpu.VMEM(full, bf16)),
        (left, wide),
        {4: 0},
        spaces=(SM,),
    )
    low_a, low_b = both_sides(low)
    part = call(
        functools.partial(own_kernel, blocks), "own_products", (low, tiles), pltpu.VMEM(full, f32)
    )
    twice, low, sums = call(
        functools.partial(second_kernel, blocks),
        "twice",
        (low_a, low_b, tiles, part, noise, vec, image),
        (
            pltpu.VMEM(full, f32),
            pltpu.VMEM((width, local_rows + 3 * LANES), bf16),
            pltpu.VMEM((width, LANES), f32),
        ),
        (wide,),
    )
    low_a = first_side(low)
    low_b = second_side(
        call(functools.partial(copy_kernel, local_rows), "second_message", (low,), pltpu.VMEM(full, bf16))
    )
    low, low_a = lax.optimization_barrier((low, low_a))
    sums = total_over_points(sums, low_a)
    part = call(functools.partial(own_kernel, blocks), "own_products_last", (low, tiles), pltpu.VMEM(full, f32))
    prods = call(
        functools.partial(third_kernel, blocks),
        "products",
        (low_a, low_b, tiles, part),
        pltpu.VMEM(full, f32),
        (wide,),
    )
    out = jax.ShapeDtypeStruct(full, f32)
    return call(last_kernel, "update", (sums, noise, vec, image, twice, prods), (out, out, out))


def solution(mesh):
    placed = (P("pts", None), P("pts"), P("rhs", "pts"), P("pts", None))
    return jax.shard_map(
        per_device,
        mesh=mesh,
        in_specs=placed,
        out_specs=(P("rhs", "pts"), P("rhs", "pts"), P("rhs", "pts")),
        check_vma=False,
    )
```

```python
import functools

import jax
import jax.numpy as jnp
from jax import lax
from jax.experimental import pallas as pl
from jax.experimental.pallas import tpu as pltpu
from jax.sharding import PartitionSpec as P

F = 32
BLK = 128
REACH = 16
WEXP = 18
LANES = 128
GAMMA = float(WEXP) ** (1.0 / (WEXP + 1))
GAMMA_SQ = GAMMA * GAMMA
OFFSET = GAMMA * (WEXP + 1) / WEXP
TINY = 1e-30
SCALE = 1.0 / (4 * BLK)
SHIFT = 2.0 / (0.5 + 0.6)
SUMS = 9
STEPS = (48, 16, 8)
FIELD = 10
MIB = 1 << 20

f32 = jnp.float32
bf16 = jnp.bfloat16


def rounded(x):
    return x.astype(bf16).astype(f32)


def three_parts(x):
    high = rounded(x)
    rest = x - high
    middle = rounded(rest)
    return high, middle, rounded(rest - middle)


def eight_rows(rows):
    row = lax.broadcasted_iota(jnp.int32, (8, rows[0].shape[1]), 0)
    out = jnp.zeros((8, rows[0].shape[1]), f32)
    for at, value in enumerate(rows):
        out = jnp.where(row == at, value, out)
    return out


def fill_features(points, left_ref, first, right_ref=None):
    x = points.astype(f32)
    count = x.shape[1]
    squares = three_parts(GAMMA_SQ * jnp.sum(x * x, axis=0, keepdims=True))
    ones = [jnp.ones((1, count), f32)] * 3
    blank = jnp.zeros((LANES - 3 * F - 8, count), f32)
    left = jnp.concatenate([x, x, x, eight_rows(list(squares) + ones), blank], axis=0).astype(bf16)
    for b in range(count // BLK):
        left_ref[first + b] = left[:, b * BLK : (b + 1) * BLK].T
    if right_ref is not None:
        cross = three_parts((-2.0 * GAMMA_SQ) * x)
        right = jnp.concatenate(list(cross) + [eight_rows(ones + list(squares)), blank], axis=0).astype(bf16)
        for b in range(count // BLK):
            right_ref[b] = right[:, b * BLK : (b + 1) * BLK]


def tile_values(left, right):
    scaled = jnp.dot(left, right, preferred_element_type=f32)
    scaled = jnp.maximum(scaled, TINY)
    s = jnp.maximum(GAMMA - scaled * lax.rsqrt(scaled), 0.0)
    s2 = s * s
    s4 = s2 * s2
    s8 = s4 * s4
    s16 = s8 * s8
    return ((s16 * s2) * (OFFSET - s)).astype(bf16)


def entry(slot, mirror, other, home):
    return (((((home << 5) + other) << FIELD) + mirror) << FIELD) + slot


def make_tiles(first, count, list_ref, left_ref, right_ref, tiles_ref, mirrored):
    mask = (1 << FIELD) - 1

    def one(at):
        code = list_ref[first + at]
        home = code >> (2 * FIELD + 5)
        other = (code >> (2 * FIELD)) & 31
        tile = tile_values(left_ref[other], right_ref[home])
        if mirrored:
            tiles_ref[(code >> FIELD) & mask] = tile.T
        tiles_ref[code & mask] = tile

    done = jnp.int32(0)
    for size in STEPS:

        def step(at, carry, size=size, done=done):
            for k in range(size):
                one(done + at * size + k)
            return carry

        last = size == STEPS[-1]
        steps = (count - done + (size - 1 if last else 0)) // size
        lax.fori_loop(0, steps, step, 0)
        done = done + steps * size


def local_slot(blocks, home, other):
    return ((home // 2) * blocks + other) * 2 + home % 2


def side_slot(blocks, home, other, after):
    wide = other - 2 * (home // 2) + (blocks if after else 0)
    return blocks * blocks + ((home // 2) * (blocks + 2) + wide) * 2 + home % 2


def spare_slot(blocks):
    return 2 * blocks * (blocks + 1)


def local_entries(blocks):
    return [(a, b, REACH + b - a) for a in range(blocks) for b in range(a, blocks)]


def side_entries(blocks, after):
    if after:
        return [(a, b, 2 * REACH + b - a) for a in range(blocks) for b in range(a + 1)]
    return [(a, b, b - a) for a in range(blocks) for b in range(a, blocks)]


def pad_list(end, list_ref, spare):
    for k in range(STEPS[-1] - 1):
        list_ref[end + k] = jnp.int32(entry(spare, spare, 0, 0))


def clear_tiles(first, last, list_ref, tiles_ref, mirrored):
    mask = (1 << FIELD) - 1

    def step(at, carry):
        code = list_ref[at]
        tiles_ref[code & mask] = jnp.zeros((BLK, BLK), bf16)
        if mirrored:
            tiles_ref[(code >> FIELD) & mask] = jnp.zeros((BLK, BLK), bf16)
        return carry

    lax.fori_loop(first, last, step, 0)


def products(vec, tiles_ref, first, wide):
    tiles = tiles_ref[first : first + 2 * wide].reshape(wide, 2, BLK, BLK)
    tiles = jnp.concatenate([tiles[:, 0].reshape(wide * BLK, BLK), tiles[:, 1].reshape(wide * BLK, BLK)], axis=1)
    return jnp.dot(vec, tiles, preferred_element_type=f32)


def pair_cols(pair):
    return slice(pair * 2 * BLK, (pair + 1) * 2 * BLK)


def local_products(blocks, vec, tiles_ref, out_ref):
    for pair in range(blocks // 2):
        out_ref[:, pair_cols(pair)] = products(vec, tiles_ref, pair * 2 * blocks, blocks)


def gather_sides(blocks, before, side_a, side_b, wide_ref):
    size = blocks * BLK
    at_a = pl.multiple_of(jnp.where(before == 1, 0, size), size)
    at_b = pl.multiple_of(size - at_a, size)
    wide_ref[:, pl.ds(at_a, size)] = side_a
    wide_ref[:, pl.ds(at_b, size)] = side_b


def side_products(blocks, pair, wide_ref, tiles_ref):
    vec = wide_ref[:, pair * 2 * BLK : (pair * 2 + blocks + 2) * BLK]
    return products(vec, tiles_ref, blocks * blocks + pair * 2 * (blocks + 2), blocks + 2)


def odd_place():
    return lax.rem(lax.axis_index("pts"), 2)


def prep_kernel(points_ref, vec_ref, noise_ref, pattern_ref, out_ref, near_vec_ref, near_noise_ref, listed_ref, sems):
    points_copy = pltpu.make_async_copy(points_ref, out_ref.at[:F], sems.at[0])
    vec_copy = pltpu.make_async_copy(vec_ref, near_vec_ref, sems.at[1])
    noise_copy = pltpu.make_async_copy(noise_ref, near_noise_ref, sems.at[2])
    vec_copy.start()
    points_copy.start()
    noise_copy.start()
    pattern_copy = pltpu.make_async_copy(pattern_ref, listed_ref, sems.at[3])
    pattern_copy.start()
    vec_copy.wait()
    out_ref[F:, :] = near_vec_ref[...].astype(bf16)
    points_copy.wait()
    noise_copy.wait()
    pattern_copy.wait()


def local_kernel(
    blocks, listed_ref, own_ref, tiles_ref, right_ref, part_ref, side_list_ref, left_ref, list_ref
):
    fill_features(own_ref[:F, :], left_ref, 0, right_ref)
    for pair in range(blocks // 2):
        first = blocks * blocks + pair * 2 * (blocks + 2)
        tiles_ref[first + 1] = jnp.zeros((BLK, BLK), bf16)
        tiles_ref[first + 2 * (blocks + 1)] = jnp.zeros((BLK, BLK), bf16)
    entries = [
        (entry(local_slot(blocks, home, other), local_slot(blocks, other, home), other, home), home, column)
        for home, other, column in local_entries(blocks)
    ]
    count = scan_entries(entries, listed_ref, list_ref, 0)
    clear_tiles(count + STEPS[-1], list_ref.shape[0], list_ref, tiles_ref, True)
    pad_list(count, list_ref, spare_slot(blocks))
    make_tiles(0, count, list_ref, left_ref, right_ref, tiles_ref, True)
    for row, after in enumerate((True, False)):
        entries = []
        for home, other, column in side_entries(blocks, after):
            slot = side_slot(blocks, home, other, after)
            entries.append((entry(slot, slot, other, home), home, column))
        size = len(entries) + STEPS[-1]
        side_count = scan_entries(entries, listed_ref, side_list_ref, row * size)
        side_list_ref[2 * size + row] = side_count
        pad_list(row * size + side_count, side_list_ref, spare_slot(blocks))
    local_products(blocks, own_ref[F:, :], tiles_ref, part_ref)


def scan_entries(entries, listed_ref, list_ref, first):
    size = len(entries) + STEPS[-1]
    count = jnp.int32(0)
    for at, (code, home, column) in enumerate(entries):
        live = listed_ref[home, column]
        list_ref[first + jnp.where(live == 1, count, size - 1 - at + count)] = jnp.int32(code)
        count = count + live
    return count


def make_side(blocks, before, side_list_ref, points, right_ref, tiles_ref, left_ref):
    size = blocks * (blocks + 1) // 2 + STEPS[-1]
    first = before * size
    count = side_list_ref[2 * size + before]
    clear_tiles(first + count + STEPS[-1], first + size, side_list_ref, tiles_ref, False)
    fill_features(points, left_ref, 0)
    make_tiles(first, count, side_list_ref, left_ref, right_ref, tiles_ref, False)


def side_kernel(blocks, side_list_ref, b_ref, right_ref, tiles_in, tiles_ref, left_ref):
    del tiles_in
    make_side(blocks, 1 - odd_place(), side_list_ref, b_ref[:F, :], right_ref, tiles_ref, left_ref)


def first_kernel(
    blocks, side_list_ref, a_ref, b_ref, right_ref, tiles_in, part_ref, noise_ref, vec_ref,
    tiles_ref, image_ref, low_ref, left_ref, wide_ref,
):
    del tiles_in
    before = odd_place()
    make_side(blocks, before, side_list_ref, a_ref[:F, :], right_ref, tiles_ref, left_ref)
    gather_sides(blocks, before, a_ref[F:, :], b_ref[F:, :], wide_ref)
    for pair in range(blocks // 2):
        cols = pair_cols(pair)
        total = part_ref[:, cols] + side_products(blocks, pair, wide_ref, tiles_ref)
        image = noise_ref[:, cols] * vec_ref[:, cols] + total * SCALE
        image_ref[:, cols] = image
        low_ref[:, cols] = image.astype(bf16)


def own_kernel(blocks, own_ref, tiles_ref, part_ref):
    local_products(blocks, own_ref[:, : blocks * BLK], tiles_ref, part_ref)


def copy_kernel(columns, from_ref, to_ref):
    to_ref[...] = from_ref[:, :columns]


def second_kernel(
    blocks, a_ref, b_ref, tiles_ref, part_ref, noise_ref, vec_ref, image_ref,
    twice_ref, low_ref, sums_ref, wide_ref,
):
    width = vec_ref.shape[0]
    gather_sides(blocks, odd_place(), a_ref[...], b_ref[...], wide_ref)
    totals = [jnp.zeros((width, LANES), f32) for _ in range(SUMS)]
    for pair in range(blocks // 2):
        cols = pair_cols(pair)
        r = vec_ref[:, cols]
        w = image_ref[:, cols]
        q = noise_ref[:, cols] * w + (part_ref[:, cols] + side_products(blocks, pair, wide_ref, tiles_ref)) * SCALE
        twice_ref[:, cols] = q
        u = r - SHIFT * w
        y = w - SHIFT * q
        low_ref[:, cols] = y.astype(bf16)
        terms = (r * r, r * w, u * u, u * w, w * w, y * u, q * u, y * w, q * w)
        totals = [total + (term[:, :LANES] + term[:, LANES:]) for total, term in zip(totals, terms)]
    lane = lax.broadcasted_iota(jnp.int32, (width, LANES), 1)
    out = jnp.zeros((width, LANES), f32)
    for at, total in enumerate(totals):
        out = jnp.where(lane == at, jnp.sum(total, axis=1, keepdims=True), out)
    sums_ref[...] = out
    points = blocks * BLK
    for at, part in enumerate(three_parts(out)):
        low_ref[:, points + at * LANES : points + (at + 1) * LANES] = part.astype(bf16)


def third_kernel(blocks, a_ref, b_ref, tiles_ref, part_ref, out_ref, wide_ref):
    points = blocks * BLK
    gather_sides(blocks, odd_place(), a_ref[:, :points], b_ref[...], wide_ref)
    for pair in range(blocks // 2):
        cols = pair_cols(pair)
        out_ref[:, cols] = (part_ref[:, cols] + side_products(blocks, pair, wide_ref, tiles_ref)) * SCALE


def last_kernel(sums_ref, noise_ref, vec_ref, image_ref, twice_ref, prod_ref, x_ref, r_ref, w_ref, held_ref, sems):
    width, points = vec_ref.shape
    rr, rw, uu, uw, ww, yu, qu, yw, qw = [
        jnp.broadcast_to(sums_ref[:, at : at + 1], (width, LANES)) for at in range(SUMS)
    ]
    alpha0 = rr / rw
    delta = alpha0 - SHIFT
    norm = uu - 2.0 * delta * uw + delta * delta * ww
    curv = yu - delta * (qu + yw) + delta * delta * qw
    beta = norm / rr
    alpha1 = norm / (curv - beta * norm / alpha0)
    share = alpha0 * (1.0 / SHIFT)
    copies = []
    for at in range(0, points, LANES):
        cols = slice(at, at + LANES)
        r0, w0, q0, noise = vec_ref[:, cols], image_ref[:, cols], twice_ref[:, cols], noise_ref[:, cols]
        r1 = r0 - alpha0 * w0
        w1 = w0 - alpha0 * q0
        q1 = noise * w1 + (1.0 - share) * (q0 - noise * w0) + share * prod_ref[:, cols]
        held_ref[0, :, cols] = alpha0 * r0 + alpha1 * (r1 + beta * r0)
        held_ref[1, :, cols] = r1 - alpha1 * (w1 + beta * w0)
        held_ref[2, :, cols] = w1 - alpha1 * (q1 + beta * q0)
        if (at + LANES) % (points // 2) == 0:
            half = slice(at + LANES - points // 2, at + LANES)
            for k, ref in enumerate((x_ref, r_ref, w_ref)):
                copies.append(pltpu.make_async_copy(held_ref.at[k, :, half], ref.at[:, half], sems.at[len(copies)]))
                copies[-1].start()
    for copy in copies:
        copy.wait()


def swap_pairs(count, first):
    pairs = []
    for low in range(first, count - 1, 2):
        pairs += [(low, low + 1), (low + 1, low)]
    return pairs


def first_side(x):
    return lax.ppermute(x, "pts", swap_pairs(lax.axis_size("pts"), 0))


def second_side(x):
    return lax.ppermute(x, "pts", swap_pairs(lax.axis_size("pts"), 1))


def both_sides(x):
    return first_side(x), second_side(x)


def total_over_points(x, neighbour):
    count = lax.axis_size("pts")
    if count & (count - 1):
        return lax.psum(x, "pts")
    if count == 1:
        return x
    high, middle, low = [
        neighbour[:, neighbour.shape[1] - (3 - k) * LANES :][:, :LANES].astype(f32) for k in range(3)
    ]
    x = x + ((high + middle) + low)
    step = 2
    while step < count:
        x = x + lax.ppermute(x, "pts", [(i, i ^ step) for i in range(count)])
        step *= 2
    return x


VM = pl.BlockSpec(memory_space=pltpu.VMEM)
FAR = pl.BlockSpec(memory_space=pltpu.HBM)
SM = pl.BlockSpec(memory_space=pltpu.SMEM)


def per_device(points, noise_var, right_side, pattern):
    local_rows = points.shape[0]
    width = right_side.shape[0]
    blocks = local_rows // BLK
    assert blocks == REACH
    params = pltpu.CompilerParams(vmem_limit_bytes=12 * MIB)
    full = (width, local_rows)
    tiles_type = pltpu.VMEM((spare_slot(blocks) + 1, BLK, BLK), bf16)
    pairs = blocks * (blocks + 1) // 2

    def numbers(count):
        return pltpu.SMEM((count,), jnp.int32)

    left = pltpu.VMEM((blocks, BLK, LANES), bf16)
    wide = pltpu.VMEM((width, 2 * local_rows), bf16)

    def call(kernel, name, ins, outs, scratch=(), aliases=None, spaces=(), out_space=VM):
        spaces = tuple(spaces) + (VM,) * (len(ins) - len(spaces))
        return pl.pallas_call(
            kernel,
            out_shape=outs,
            in_specs=list(spaces),
            out_specs=jax.tree.map(
                lambda x: SM if x.dtype == jnp.int32 else out_space, outs, is_leaf=lambda x: hasattr(x, "dtype")
            ),
            scratch_shapes=list(scratch),
            input_output_aliases=aliases or {},
            compiler_params=params,
            cost_estimate=pl.CostEstimate(flops=10**9, bytes_accessed=10**7, transcendentals=0),
            name=name,
        )(*[pltpu.with_memory_space_constraint(x, space.memory_space) for x, space in zip(ins, spaces)])

    payload, vec, noise, listed = call(
        prep_kernel,
        "prep",
        (points.T, right_side, noise_var[None, :], pattern),
        (
            pltpu.VMEM((F + width, local_rows), bf16),
            pltpu.VMEM(full, f32),
            pltpu.VMEM((1, local_rows), f32),
            pltpu.SMEM(pattern.shape, jnp.int32),
        ),
        (pltpu.SemaphoreType.DMA((4,)),),
        spaces=(FAR,) * 4,
    )
    halo_a, halo_b = both_sides(payload)
    tiles, right, part, side_list = call(
        functools.partial(local_kernel, blocks),
        "local_tiles",
        (listed, payload),
        (
            tiles_type,
            pltpu.VMEM((blocks, LANES, BLK), bf16),
            pltpu.VMEM(full, f32),
            numbers(2 * (pairs + STEPS[-1]) + 2),
        ),
        (left, numbers(pairs + STEPS[-1])),
        spaces=(SM,),
    )
    tiles = call(
        functools.partial(side_kernel, blocks),
        "side_tiles",
        (side_list, halo_b, right, tiles),
        tiles_type,
        (left,),
        {3: 0},
        spaces=(SM,),
    )
    tiles, image, low = call(
        functools.partial(first_kernel, blocks),
        "image",
        (side_list, halo_a, halo_b, right, tiles, part, noise, vec),
        (tiles_type, pltpu.VMEM(full, f32), pltpu.VMEM(full, bf16)),
        (left, wide),
        {4: 0},
        spaces=(SM,),
    )
    low_a, low_b = both_sides(low)
    part = call(
        functools.partial(own_kernel, blocks), "own_products", (low, tiles), pltpu.VMEM(full, f32)
    )
    twice, low, sums = call(
        functools.partial(second_kernel, blocks),
        "twice",
        (low_a, low_b, tiles, part, noise, vec, image),
        (
            pltpu.VMEM(full, f32),
            pltpu.VMEM((width, local_rows + 3 * LANES), bf16),
            pltpu.VMEM((width, LANES), f32),
        ),
        (wide,),
    )
    low_a = first_side(low)
    low_b = second_side(
        call(functools.partial(copy_kernel, local_rows), "second_message", (low,), pltpu.VMEM(full, bf16))
    )
    low, low_a = lax.optimization_barrier((low, low_a))
    sums = total_over_points(sums, low_a)
    part = call(functools.partial(own_kernel, blocks), "own_products_last", (low, tiles), pltpu.VMEM(full, f32))
    prods = call(
        functools.partial(third_kernel, blocks),
        "products",
        (low_a, low_b, tiles, part),
        pltpu.VMEM(full, f32),
        (wide,),
    )
    out = jax.ShapeDtypeStruct(full, f32)
    return call(
        last_kernel,
        "update",
        (sums, noise, vec, image, twice, prods),
        (out, out, out),
        (pltpu.VMEM((3,) + full, f32), pltpu.SemaphoreType.DMA((6,))),
        out_space=FAR,
    )


def solution(mesh):
    placed = (P("pts", None), P("pts"), P("rhs", "pts"), P("pts", None))
    return jax.shard_map(
        per_device,
        mesh=mesh,
        in_specs=placed,
        out_specs=(P("rhs", "pts"), P("rhs", "pts"), P("rhs", "pts")),
        check_vma=False,
    )
```
